256 devices in a mesh: tower: 16 (over x, y), shard: 16 (over z, core).
Axes of the slice: x: 4, y: 4, z: 8, core: 2. Of those that a mesh axis runs over, the one named last changes fastest.
Arguments:
- pooled: bfloat16 [16, 6144, 48, 128], P('tower', None, 'shard'), may hold values from -6 to 6
- cross_down: bfloat16 [16, 2, 4096, 512], P('tower', None, 'shard'), may hold values from -0.09375 to 0.09375
- cross_up: bfloat16 [16, 2, 512, 4096], P('tower', None, None, 'shard'), may hold values from -0.25 to 0.25
- cross_bias: bfloat16 [16, 2, 4096], P('tower'), may hold values from -3 to 3
- comp_weight: bfloat16 [16, 4096, 256], P('tower', 'shard'), may hold values from -0.09375 to 0.09375
- comp_bias: bfloat16 [16, 256], P('tower'), may hold values from -3 to 3
- over_weight: bfloat16 [4096, 1024], P('tower', 'shard'), may hold values from -0.09375 to 0.09375
- over_bias: bfloat16 [1024], replicated, may hold values from -3 to 3
- table_tower: int32 [512], replicated, may hold values from 0 to 15, as said below
- table_owner: int32 [512], replicated, may hold values from 0 to 15, as said below
Outputs:
- scores: bfloat16 [16, 384, 1024], P('shard', 'tower')
The draws below stay inside these ranges and needn't reach their ends.
Inputs may be any that keep to these rules, and one draw needn't show every extreme that they name: `table_tower`: each value names exactly 32 tables. `table_owner`: among the tables of one tower no value is named by more than 3 tables, and in every tower some value is named by exactly 3.
All inputs are finite; a program needn't handle non-finite values.
Results may differ from the reference program's by a relative error of at most 0.014.
Values may be sent and summed in bfloat16 or wider, within the bound.
No kernel may reach another device: no remote copies, remote signals or barrier semaphores. Data moves between devices by JAX's collectives and lax.ppermute only.
A program may use at most 128 MiB of HBM per device.

```python
import jax
import jax.numpy as jnp
from jax import lax

EMB = 128
TPT = 32
RANK = 512
CMP = 256
OUT = 1024
LAYERS = 2
SMP_DEV = 384
TOWERS = 16
TABLES = 512
F = 4096
CAT = 4096
TAB_MOST = 3
SLOTS = 48
BATCH = 6144
N_TOWER = 16
N_SHARD = 16


def placement_order(key):
    return jax.random.permutation(jax.random.fold_in(key, 11), TABLES).astype(jnp.int32)


def draw_table_tower(key, part):
    order = placement_order(key)
    return (order // TPT).astype(jnp.int32)


def draw_table_owner(key, part):
    order = placement_order(key)
    tower_of = order // TPT
    position = order % TPT

    def one_tower(tower_key):
        first_key, second_key = jax.random.split(tower_key)
        full_owner = jax.random.randint(first_key, (), 0, SLOTS // TAB_MOST)
        slot_ids = jnp.arange(SLOTS, dtype=jnp.int32)
        owners = slot_ids // TAB_MOST
        scores = jax.random.permutation(second_key, SLOTS).astype(jnp.int32)
        scores = jnp.where(owners == full_owner, slot_ids % TAB_MOST - TAB_MOST, scores)
        chosen = jnp.argsort(scores)[:TPT]
        return (chosen // TAB_MOST).astype(jnp.int32)
    tower_keys = jax.random.split(jax.random.fold_in(key, 23), TOWERS)
    assigned = jax.vmap(one_tower)(tower_keys)
    return assigned[tower_of, position].astype(jnp.int32)


def level_of(key, shape, cuts, smallest, top_value):
    def one(dim, blocks):
        steps = jax.random.uniform(jax.random.fold_in(jax.random.fold_in(key, 6), dim), (blocks,), jnp.float32, smallest / len(cuts), top_value / len(cuts))
        return jnp.repeat(jnp.exp(steps), shape[dim] // blocks).reshape((-1,) + (1,) * (len(shape) - dim - 1))

    factor_of = one(*cuts[0])
    for cut in cuts[1:]:
        factor_of = factor_of * one(*cut)
    return factor_of


def noise(stream_key, extent, width, reach, cuts=(), kind=jnp.bfloat16):
    array = width * jax.random.normal(stream_key, extent, jnp.float32)
    if cuts:
        array = array * level_of(stream_key, extent, cuts, -0.22, 0.18)
    return jnp.clip(array, -reach, reach).astype(kind)


def setup_inputs(seed: int = 0) -> dict:
    arg_keys = jax.random.split(jax.random.key(seed), 11)
    return {
        "pooled": noise(arg_keys[0], (TOWERS, BATCH, SLOTS, EMB), 1.0, 6.0, ((0, 16), (2, 16))),
        "cross_down": noise(arg_keys[1], (TOWERS, LAYERS, F, RANK), F ** -0.5, 0.09375, ((0, 16), (2, 16))),
        "cross_up": noise(arg_keys[2], (TOWERS, LAYERS, RANK, F), RANK ** -0.5, 0.25, ((0, 16), (3, 16))),
        "cross_bias": noise(arg_keys[3], (TOWERS, LAYERS, F), 0.5, 3.0, ((0, 16),)),
        "comp_weight": noise(arg_keys[4], (TOWERS, F, CMP), F ** -0.5, 0.09375, ((0, 16), (1, 16))),
        "comp_bias": noise(arg_keys[5], (TOWERS, CMP), 0.5, 3.0, ((0, 16),)),
        "over_weight": noise(arg_keys[6], (CAT, OUT), CAT ** -0.5, 0.09375, ((0, 16), (1, 16))),
        "over_bias": noise(arg_keys[7], (OUT,), 0.5, 3.0),
        "table_tower": draw_table_tower(jax.random.fold_in(arg_keys[10], 71), 0),
        "table_owner": draw_table_owner(jax.random.fold_in(arg_keys[10], 71), 0),
    }


def slot_order(table_tower, table_owner, tower_id):
    index = jnp.arange(TABLES, dtype=jnp.int32)
    inside = table_tower == tower_id
    earlier = index[None, :] < index[:, None]
    before = inside[None, :] & earlier
    position_in = jnp.sum(before.astype(jnp.int32), axis=1).astype(jnp.int32)
    same_owner = table_owner[None, :] == table_owner[:, None]
    own_slot = jnp.sum((before & same_owner).astype(jnp.int32), axis=1).astype(jnp.int32)
    wanted = (table_owner * TAB_MOST + own_slot).astype(jnp.int32)
    picked = inside[None, :] & (position_in[None, :] == jnp.arange(TPT, dtype=jnp.int32)[:, None])
    return jnp.sum(jnp.where(picked, wanted[None, :], 0), axis=1).astype(jnp.int32)


def reference(pooled, cross_down, cross_up, cross_bias, comp_weight, comp_bias, over_weight, over_bias, table_tower, table_owner):
    def one_tower(tower_id):
        wanted = slot_order(table_tower, table_owner, tower_id)
        tables = jnp.take(pooled[tower_id], wanted, axis=1)
        base = tables.reshape(BATCH, F)
        state = base
        for section_index in range(LAYERS):
            lowered = jnp.dot(state, cross_down[tower_id, section_index], preferred_element_type=jnp.float32).astype(jnp.bfloat16)
            raised = jnp.dot(lowered, cross_up[tower_id, section_index], preferred_element_type=jnp.float32)
            state = (base.astype(jnp.float32) * (raised + cross_bias[tower_id, section_index].astype(jnp.float32)) + state.astype(jnp.float32)).astype(jnp.bfloat16)
        squeezed = jnp.dot(state, comp_weight[tower_id], preferred_element_type=jnp.float32) + comp_bias[tower_id].astype(jnp.float32)
        return squeezed.astype(jnp.bfloat16)

    towers_out = lax.map(one_tower, jnp.arange(N_TOWER, dtype=jnp.int32))
    joined = jnp.transpose(towers_out, (1, 0, 2)).reshape(BATCH, CAT)
    mixed = jnp.dot(joined, over_weight, preferred_element_type=jnp.float32) + over_bias.astype(jnp.float32)
    return jax.nn.relu(mixed).astype(jnp.bfloat16).reshape(N_SHARD, SMP_DEV, OUT)
```

```python
import jax
import jax.numpy as jnp
from jax import lax
from jax.experimental import pallas as pl
from jax.experimental.pallas import tpu as pltpu
from jax.sharding import PartitionSpec as P

F32 = jnp.float32
BF16 = jnp.bfloat16


def slot_order(table_tower, table_owner, tower_id, per_tower, slot_most):
    table_count = table_tower.shape[0]
    index = jnp.arange(table_count, dtype=jnp.int32)
    inside = table_tower == tower_id
    earlier = index[None, :] < index[:, None]
    before = inside[None, :] & earlier
    position_in = jnp.sum(before.astype(jnp.int32), axis=1)
    same_owner = table_owner[None, :] == table_owner[:, None]
    own_slot = jnp.sum((before & same_owner).astype(jnp.int32), axis=1)
    wanted = table_owner * slot_most + own_slot
    picked = inside[None, :] & (
        position_in[None, :] == jnp.arange(per_tower, dtype=jnp.int32)[:, None]
    )
    return jnp.sum(jnp.where(picked, wanted[None, :], 0), axis=1)


def tower_kernel(
    slots, received, gathered, bias, comp_bias, over_rows, out, base, state, down0, down1, up, comp, sems
):
    rows, features = base.shape
    width = comp.shape[-1]
    shards, rank = up.shape[0], down0.shape[-1]
    step = features // shards
    for p in range(features // 128):
        pltpu.make_async_copy(
            received.at[slots[p]], base.at[:, pl.ds(p * 128, 128)], sems.at[0]
        ).start()
    copies = [
        pltpu.make_async_copy(gathered.at[:, :, pl.ds(0, 32), :], down0, sems.at[1]),
        pltpu.make_async_copy(gathered.at[:, :, pl.ds(64, 64), :], up, sems.at[2]),
        pltpu.make_async_copy(gathered.at[:, :, pl.ds(32, 32), :], down1, sems.at[3]),
    ] + [
        pltpu.make_async_copy(
            gathered.at[:, :, pl.ds(128, 16), pl.ds(half * width, width)],
            comp.at[:, half],
            sems.at[4 + half],
        )
        for half in range(2)
    ]
    for copy in copies:
        copy.start()
    pltpu.make_async_copy(base, base, sems.at[0]).wait()
    copies[0].wait()
    raise_by = up.reshape(shards, up.shape[1] * up.shape[2], up.shape[3])
    lowered = jnp.dot(
        base[...], down0.reshape(features, rank)[...], preferred_element_type=F32
    ).astype(BF16)
    copies[1].wait()
    for layer in range(2):
        for s in range(shards):
            here = pl.ds(s * step, step)
            raised = jnp.dot(
                lowered, raise_by[s, :, pl.ds(layer * step, step)], preferred_element_type=F32
            )
            part = base[:, here].astype(F32)
            held = part if layer == 0 else state[:, here].astype(F32)
            state[:, here] = (part * (raised + bias[layer : layer + 1, here]) + held).astype(BF16)
        if layer == 0:
            copies[2].wait()
            lowered = jnp.dot(
                state[...], down1.reshape(features, rank)[...], preferred_element_type=F32
            ).astype(BF16)
    copies[3].wait()
    copies[4].wait()
    squeezed = jnp.dot(state[...], comp.reshape(features, width)[...], preferred_element_type=F32)
    squeezed = (squeezed + comp_bias[...]).astype(BF16)
    out[...] = jnp.dot(squeezed, over_rows[...], preferred_element_type=F32).astype(BF16)


def on_device(
    pooled,
    cross_down,
    cross_up,
    cross_bias,
    comp_weight,
    comp_bias,
    over_weight,
    over_bias,
    table_tower,
    table_owner,
):
    tower_id = lax.axis_index("tower")
    shards, towers = lax.axis_size("shard"), lax.axis_size("tower")
    _, batch, slot_most, emb = pooled.shape
    layers, rank, step = cross_up.shape[1:]
    features = step * shards
    width = comp_weight.shape[2]
    samples = batch // shards
    outputs = over_weight.shape[1] * shards

    down_part = cross_down[0].reshape(layers, 8, step // 8, rank).transpose(1, 0, 2, 3)
    up_part = cross_up[0].transpose(1, 0, 2).reshape(8, rank // 8, layers * step)
    comp_part = comp_weight[0].reshape(2, step // 2, width).transpose(1, 0, 2)
    packed = jnp.concatenate(
        [
            down_part.reshape(8, layers * step // 8, rank),
            up_part,
            comp_part.reshape(8, step // 16, 2 * width),
        ],
        axis=1,
    )
    gathered = lax.all_gather(packed, "shard", axis=0)
    by_slot = pooled[0].transpose(1, 0, 2).reshape(slot_most, shards, samples, emb)
    received = lax.all_to_all(
        by_slot.transpose(1, 0, 2, 3), "shard", split_axis=0, concat_axis=0, tiled=True
    ).reshape(shards * slot_most, samples, emb)
    over_rows = lax.all_gather(over_weight, "shard", axis=1, tiled=True)
    slots = slot_order(table_tower, table_owner, tower_id, features // emb, slot_most)

    partial = pl.pallas_call(
        tower_kernel,
        grid_spec=pltpu.PrefetchScalarGridSpec(
            num_scalar_prefetch=1,
            grid=(1,),
            in_specs=[
                pl.BlockSpec(memory_space=pl.ANY),
                pl.BlockSpec(memory_space=pl.ANY),
                pl.BlockSpec((layers, features), lambda i, *_: (0, 0)),
                pl.BlockSpec((1, width), lambda i, *_: (0, 0)),
                pl.BlockSpec((width, outputs), lambda i, *_: (0, 0)),
            ],
            out_specs=pl.BlockSpec((samples, outputs), lambda i, *_: (0, 0)),
            scratch_shapes=[
                pltpu.VMEM((samples, features), BF16),
                pltpu.VMEM((samples, features), BF16),
                pltpu.VMEM((shards, 8, step // 8, rank), BF16),
                pltpu.VMEM((shards, 8, step // 8, rank), BF16),
                pltpu.VMEM((shards, 8, rank // 8, layers * step), BF16),
                pltpu.VMEM((shards, 2, 8, step // 16, width), BF16),
                pltpu.SemaphoreType.DMA((6,)),
            ],
        ),
        out_shape=jax.ShapeDtypeStruct((samples, outputs), BF16),
        compiler_params=pltpu.CompilerParams(vmem_limit_bytes=48 * 2**20),
        cost_estimate=pl.CostEstimate(flops=8 * 10**9, bytes_accessed=24 * 10**6, transcendentals=0),
    )(
        slots,
        received,
        gathered,
        cross_bias[0].astype(F32),
        comp_bias.astype(F32),
        over_rows,
    )
    summed = lax.all_to_all(
        partial.reshape(towers, samples // towers, outputs), "tower", 0, 0, tiled=True
    )
    total = jnp.sum(summed.astype(F32), axis=0) + over_bias.astype(F32)
    return jax.nn.relu(total).astype(BF16)[None]


def solution(mesh):
    placed = (
        P("tower", None, "shard", None),
        P("tower", None, "shard", None),
        P("tower", None, None, "shard"),
        P("tower", None, None),
        P("tower", "shard", None),
        P("tower", None),
        P("tower", "shard"),
        P(),
        P(),
        P(),
    )
    return jax.shard_map(
        on_device, mesh=mesh, in_specs=placed, out_specs=P("shard", "tower", None), check_vma=False
    )
```

```python
import jax
import jax.numpy as jnp
from jax import lax
from jax.experimental import pallas as pl
from jax.experimental.pallas import tpu as pltpu
from jax.sharding import PartitionSpec as P

F32 = jnp.float32
BF16 = jnp.bfloat16


def slot_order(table_tower, table_owner, tower_id, per_tower, slot_most):
    table_count = table_tower.shape[0]
    index = jnp.arange(table_count, dtype=jnp.int32)
    inside = table_tower == tower_id
    earlier = index[None, :] < index[:, None]
    before = inside[None, :] & earlier
    position_in = jnp.sum(before.astype(jnp.int32), axis=1)
    same_owner = table_owner[None, :] == table_owner[:, None]
    own_slot = jnp.sum((before & same_owner).astype(jnp.int32), axis=1)
    wanted = table_owner * slot_most + own_slot
    picked = inside[None, :] & (
        position_in[None, :] == jnp.arange(per_tower, dtype=jnp.int32)[:, None]
    )
    return jnp.sum(jnp.where(picked, wanted[None, :], 0), axis=1)


def tower_kernel(places, *refs):
    n_chunks = len(refs) - 15
    received, refs = refs[:n_chunks], refs[n_chunks:]
    gathered, refs = refs[:4], refs[4:]
    bias, comp_bias, over_rows, out, base, state, down0, down1, up, comp, sems = refs
    rows, features = base.shape
    width, rank = comp.shape[-1], down0.shape[-1]
    shards = 2 * up.shape[0]
    step, tables, chunk = features // shards, features // 128, rows // n_chunks
    core, half = places[tables], places[tables + 1]

    for i in range(n_chunks):
        for p in range(tables):
            pltpu.make_async_copy(
                received[i].at[places[p]],
                base.at[pl.ds(i * chunk, chunk), pl.ds(p * 128, 128)],
                sems.at[0],
            ).start()

    def bring(target, first, count, sem):
        for n in range(4):
            c = core if n < 2 else 1 - core
            p = half if n % 2 == 0 else 1 - half
            for x in range(4):
                pltpu.make_async_copy(
                    gathered[n].at[x, :, pl.ds(first, count), :],
                    target.at[:, c, 2 * x + p],
                    sems.at[sem],
                ).start()

    bring(down0, 0, 32, 1)
    bring(up, 64, 64, 2)
    bring(down1, 32, 32, 3)
    for n in range(4):
        c = core if n < 2 else 1 - core
        p = half if n % 2 == 0 else 1 - half
        for x in range(4):
            for m in range(2):
                pltpu.make_async_copy(
                    gathered[n].at[x, :, pl.ds(128, 16), pl.ds(m * width, width)],
                    comp.at[:, c, m, 2 * x + p],
                    sems.at[4],
                ).start()

    def arrived(target, sem):
        pltpu.make_async_copy(target, target, sems.at[sem]).wait()

    arrived(base, 0)
    arrived(down0, 1)
    raise_by = up.reshape(shards, rank, 2 * step)
    lowered = jnp.dot(
        base[...], down0.reshape(features, rank)[...], preferred_element_type=F32
    ).astype(BF16)
    arrived(up, 2)
    for layer in range(2):
        for s in range(shards):
            here = pl.ds(s * step, step)
            raised = jnp.dot(
                lowered, raise_by[s, :, pl.ds(layer * step, step)], preferred_element_type=F32
            )
            part = base[:, here].astype(F32)
            held = part if layer == 0 else state[:, here].astype(F32)
            state[:, here] = (part * (raised + bias[layer : layer + 1, here]) + held).astype(BF16)
        if layer == 0:
            arrived(down1, 3)
            lowered = jnp.dot(
                state[...], down1.reshape(features, rank)[...], preferred_element_type=F32
            ).astype(BF16)
    arrived(comp, 4)
    squeezed = jnp.dot(state[...], comp.reshape(features, width)[...], preferred_element_type=F32)
    squeezed = (squeezed + comp_bias[...]).astype(BF16)
    out[...] = jnp.dot(squeezed, over_rows[...], preferred_element_type=F32).astype(BF16)


CHUNKS = 2
MEMBERS = [[4 * x + 2 * h + yb for x in range(4) for yb in range(2)] for h in range(2)]
ALONG_X = [[4 * x + y for x in range(4)] for y in range(4)]
ALONG_Z = [[2 * z + core for z in range(8)] for core in range(2)]
SWAP_Y = [(i, i ^ 1) for i in range(16)]
SWAP_HALF = [(i, i ^ 2) for i in range(16)]
SWAP_CORE = [(i, i ^ 1) for i in range(16)]


def at(array, index):
    return lax.dynamic_index_in_dim(array, index, 0, keepdims=False)


def after(array, *others):
    corner = array[(0,) * array.ndim]
    for other in others:
        seen = other[(0,) * other.ndim]
        corner = jnp.where(seen == seen, corner, 0)
    return array.at[(0,) * array.ndim].set(corner)


def half_plane(pieces, member):
    whole = jnp.zeros_like(pieces)
    whole = lax.dynamic_update_index_in_dim(whole, at(pieces, member), member, 0)
    for k in range(1, 8):
        moves = [(m[g], m[(g + k) % 8]) for m in MEMBERS for g in range(8)]
        piece = lax.ppermute(at(pieces, (member + k) % 8), "tower", moves)
        first = piece if k == 1 else first
        whole = lax.dynamic_update_index_in_dim(whole, piece, (member - k) % 8, 0)
    return whole, first


def on_device(
    pooled,
    cross_down,
    cross_up,
    cross_bias,
    comp_weight,
    comp_bias,
    over_weight,
    over_bias,
    table_tower,
    table_owner,
):
    me_t, me_s = lax.axis_index("tower"), lax.axis_index("shard")
    z, core, yb, half = me_s // 2, me_s % 2, me_t % 2, (me_t // 2) % 2
    my_tower = 4 * (z // 2) + 2 * half + z % 2
    member = 2 * (me_t // 4) + yb
    shards, towers = 16, 16
    _, batch, slot_most, emb = pooled.shape
    layers, rank, step = cross_up.shape[1:]
    features = step * shards
    width = comp_weight.shape[2]
    samples = batch // shards
    small = samples // towers
    outputs = over_weight.shape[1] * shards

    down_part = cross_down[0].reshape(layers, 8, step // 8, rank).transpose(1, 0, 2, 3)
    up_part = cross_up[0].transpose(1, 0, 2).reshape(8, rank // 8, layers * step)
    comp_part = comp_weight[0].reshape(2, step // 2, width).transpose(1, 0, 2)
    packed = jnp.concatenate(
        [
            down_part.reshape(8, layers * step // 8, rank),
            up_part,
            comp_part.reshape(8, step // 16, 2 * width),
        ],
        axis=1,
    )
    spread = lax.all_to_all(packed, "tower", 0, 0, tiled=True, axis_index_groups=MEMBERS)
    mine = lax.all_to_all(spread, "shard", 0, 0, tiled=True, axis_index_groups=ALONG_Z)
    tiny = jnp.concatenate(
        [
            over_weight.reshape(-1, 128),
            cross_bias.reshape(-1, 128),
            comp_bias.reshape(-1, 128),
        ]
    )
    over_tiles, bias_tiles = over_weight.size // 128, cross_bias.size // 128
    tiny = jnp.pad(tiny, ((0, -tiny.shape[0] % 16), (0, 0)))
    tiny = lax.all_gather(tiny, "tower", axis=0)
    blocks = pooled[0].reshape(8, 2, 4, 2, 2, small, slot_most, emb)
    blocks = blocks.transpose(2, 4, 1, 6, 0, 3, 5, 7)
    rows = samples // CHUNKS
    blocks = blocks.reshape(8, 2, slot_most, CHUNKS, rows, emb)
    spread_rows, received = [], []
    for i in range(CHUNKS):
        arrived, first_piece = half_plane(blocks[:, :, :, i], member)
        spread_rows.append(arrived)
        received.append(
            lax.all_to_all(
                spread_rows[i].reshape(shards, slot_most, rows, emb), "shard", 0, 0, tiled=True
            ).reshape(shards * slot_most, rows, emb)
        )

    other = lax.ppermute(after(mine, first_piece), "tower", SWAP_Y)
    gathered = [
        lax.all_gather(part, "tower", axis=0, axis_index_groups=ALONG_X)
        for part in (after(mine, spread_rows[0], tiny), after(other, spread_rows[1], received[0]))
    ]
    gathered = [after(part, received[-1]) for part in gathered]
    gathered = gathered + [lax.ppermute(part, "shard", SWAP_CORE) for part in gathered]

    own = at(tiny, my_tower)
    bias = own[over_tiles : over_tiles + bias_tiles].reshape(layers, features).astype(F32)
    squeeze_bias = own[over_tiles + bias_tiles :][: width // 128].reshape(1, width).astype(F32)
    over_all = tiny[:, :over_tiles].reshape(4, 2, 2, width, outputs // shards)
    over_all = lax.dynamic_index_in_dim(over_all, half, 1, keepdims=False)
    over_all = jnp.repeat(over_all.reshape(8, width, outputs // shards), 2, axis=0)
    over_rows = lax.all_to_all(after(over_all, received[-1]), "shard", 0, 0, tiled=True)
    over_rows = over_rows.transpose(1, 0, 2).reshape(width, outputs)

    slots = slot_order(table_tower, table_owner, my_tower, features // emb, slot_most)
    places = jnp.concatenate([slots, core[None], yb[None]]).astype(jnp.int32)

    whole = pl.BlockSpec(memory_space=pl.ANY)
    partial = pl.pallas_call(
        tower_kernel,
        grid_spec=pltpu.PrefetchScalarGridSpec(
            num_scalar_prefetch=1,
            grid=(1,),
            in_specs=[whole] * (CHUNKS + 4)
            + [
                pl.BlockSpec((layers, features), lambda i, *_: (0, 0)),
                pl.BlockSpec((1, width), lambda i, *_: (0, 0)),
                pl.BlockSpec((width, outputs), lambda i, *_: (0, 0)),
            ],
            out_specs=pl.BlockSpec((samples, outputs), lambda i, *_: (0, 0)),
            scratch_shapes=[
                pltpu.VMEM((samples, features), BF16),
                pltpu.VMEM((samples, features), BF16),
                pltpu.VMEM((8, 2, 8, step // 8, rank), BF16),
                pltpu.VMEM((8, 2, 8, step // 8, rank), BF16),
                pltpu.VMEM((8, 2, 8, rank // 8, layers * step), BF16),
                pltpu.VMEM((8, 2, 2, 8, step // 16, width), BF16),
                pltpu.SemaphoreType.DMA((5,)),
            ],
        ),
        out_shape=jax.ShapeDtypeStruct((samples, outputs), BF16),
        compiler_params=pltpu.CompilerParams(vmem_limit_bytes=48 * 2**20),
        cost_estimate=pl.CostEstimate(flops=8 * 10**9, bytes_accessed=24 * 10**6, transcendentals=0),
    )(places, *received, *gathered, bias, squeeze_bias, over_rows)

    summed = lax.all_to_all(
        partial.reshape(8, 2 * small, outputs), "shard", 0, 0, tiled=True, axis_index_groups=ALONG_Z
    )
    summed = jnp.sum(summed.astype(F32), axis=0).reshape(2, small, outputs)
    away = lax.ppermute(at(summed, 1 - half).astype(BF16), "tower", SWAP_HALF)
    total = at(summed, half) + away.astype(F32) + over_bias.astype(F32)
    return jax.nn.relu(total).astype(BF16)[None]


def solution(mesh):
    placed = (
        P("tower", None, "shard", None),
        P("tower", None, "shard", None),
        P("tower", None, None, "shard"),
        P("tower", None, None),
        P("tower", "shard", None),
        P("tower", None),
        P("tower", "shard"),
        P(),
        P(),
        P(),
    )
    return jax.shard_map(
        on_device, mesh=mesh, in_specs=placed, out_specs=P("shard", "tower", None), check_vma=False
    )
```

```python
import jax
import jax.numpy as jnp
from jax import lax
from jax.experimental import pallas as pl
from jax.experimental.pallas import tpu as pltpu
from jax.sharding import PartitionSpec as P

F32 = jnp.float32
BF16 = jnp.bfloat16


def slot_order(table_tower, table_owner, tower_id, per_tower, slot_most):
    table_count = table_tower.shape[0]
    index = jnp.arange(table_count, dtype=jnp.int32)
    inside = table_tower == tower_id
    earlier = index[None, :] < index[:, None]
    before = inside[None, :] & earlier
    position_in = jnp.sum(before.astype(jnp.int32), axis=1)
    same_owner = table_owner[None, :] == table_owner[:, None]
    own_slot = jnp.sum((before & same_owner).astype(jnp.int32), axis=1)
    wanted = table_owner * slot_most + own_slot
    picked = inside[None, :] & (
        position_in[None, :] == jnp.arange(per_tower, dtype=jnp.int32)[:, None]
    )
    return jnp.sum(jnp.where(picked, wanted[None, :], 0), axis=1)


def tower_kernel(
    slots, received, gathered, bias, comp_bias, over_rows, out, base, state, down0, down1, up, comp, sems
):
    rows, features = base.shape
    width = comp.shape[-1]
    shards, rank = up.shape[0], down0.shape[-1]
    step = features // shards
    for p in range(features // 128):
        pltpu.make_async_copy(
            received.at[slots[p]], base.at[:, pl.ds(p * 128, 128)], sems.at[0]
        ).start()
    copies = [
        pltpu.make_async_copy(gathered.at[:, :, pl.ds(0, 32), :], down0, sems.at[1]),
        pltpu.make_async_copy(gathered.at[:, :, pl.ds(64, 64), :], up, sems.at[2]),
        pltpu.make_async_copy(gathered.at[:, :, pl.ds(32, 32), :], down1, sems.at[3]),
    ] + [
        pltpu.make_async_copy(
            gathered.at[:, :, pl.ds(128, 16), pl.ds(half * width, width)],
            comp.at[:, half],
            sems.at[4 + half],
        )
        for half in range(2)
    ]
    for copy in copies:
        copy.start()
    pltpu.make_async_copy(base, base, sems.at[0]).wait()
    copies[0].wait()
    raise_by = up.reshape(shards, up.shape[1] * up.shape[2], up.shape[3])
    lowered = jnp.dot(
        base[...], down0.reshape(features, rank)[...], preferred_element_type=F32
    ).astype(BF16)
    copies[1].wait()
    for layer in range(2):
        for s in range(shards):
            here = pl.ds(s * step, step)
            raised = jnp.dot(
                lowered, raise_by[s, :, pl.ds(layer * step, step)], preferred_element_type=F32
            )
            part = base[:, here].astype(F32)
            held = part if layer == 0 else state[:, here].astype(F32)
            state[:, here] = (part * (raised + bias[layer : layer + 1, here]) + held).astype(BF16)
        if layer == 0:
            copies[2].wait()
            lowered = jnp.dot(
                state[...], down1.reshape(features, rank)[...], preferred_element_type=F32
            ).astype(BF16)
    copies[3].wait()
    copies[4].wait()
    squeezed = jnp.dot(state[...], comp.reshape(features, width)[...], preferred_element_type=F32)
    squeezed = (squeezed + comp_bias[...]).astype(BF16)
    out[...] = jnp.dot(squeezed, over_rows[...], preferred_element_type=F32).astype(BF16)


def tower_product(slots, received, gathered, bias, squeeze_bias, over_rows):
    rows = received.shape[1]
    layers, features = bias.shape
    width, outputs = over_rows.shape
    shards, rank = gathered.shape[0], gathered.shape[3]
    step = features // shards
    return pl.pallas_call(
        tower_kernel,
        grid_spec=pltpu.PrefetchScalarGridSpec(
            num_scalar_prefetch=1,
            grid=(1,),
            in_specs=[
                pl.BlockSpec(memory_space=pl.ANY),
                pl.BlockSpec(memory_space=pl.ANY),
                pl.BlockSpec((layers, features), lambda i, *_: (0, 0)),
                pl.BlockSpec((1, width), lambda i, *_: (0, 0)),
                pl.BlockSpec((width, outputs), lambda i, *_: (0, 0)),
            ],
            out_specs=pl.BlockSpec((rows, outputs), lambda i, *_: (0, 0)),
            scratch_shapes=[
                pltpu.VMEM((rows, features), BF16),
                pltpu.VMEM((rows, features), BF16),
                pltpu.VMEM((shards, 8, step // 8, rank), BF16),
                pltpu.VMEM((shards, 8, step // 8, rank), BF16),
                pltpu.VMEM((shards, 8, rank // 8, layers * step), BF16),
                pltpu.VMEM((shards, 2, 8, step // 16, width), BF16),
                pltpu.SemaphoreType.DMA((6,)),
            ],
        ),
        out_shape=jax.ShapeDtypeStruct((rows, outputs), BF16),
        compiler_params=pltpu.CompilerParams(vmem_limit_bytes=48 * 2**20),
        cost_estimate=pl.CostEstimate(
            flops=rows * 2 * 10**7, bytes_accessed=24 * 10**6, transcendentals=0
        ),
    )(slots, received, gathered, bias, squeeze_bias, over_rows)


def at(array, index):
    return lax.dynamic_index_in_dim(array, index, 0, keepdims=False)


def after(array, *others):
    corner = array[(0,) * array.ndim]
    for other in others:
        seen = other[(0,) * other.ndim]
        corner = jnp.where(seen == seen, corner, 0)
    return array.at[(0,) * array.ndim].set(corner)


def on_device(
    pooled,
    cross_down,
    cross_up,
    cross_bias,
    comp_weight,
    comp_bias,
    over_weight,
    over_bias,
    table_tower,
    table_owner,
):
    tower_id = lax.axis_index("tower")
    shards, towers = lax.axis_size("shard"), lax.axis_size("tower")
    _, batch, slot_most, emb = pooled.shape
    layers, rank, step = cross_up.shape[1:]
    features = step * shards
    width = comp_weight.shape[2]
    samples = batch // shards
    outputs = over_weight.shape[1] * shards

    down_part = cross_down[0].reshape(layers, 8, step // 8, rank).transpose(1, 0, 2, 3)
    up_part = cross_up[0].transpose(1, 0, 2).reshape(8, rank // 8, layers * step)
    comp_part = comp_weight[0].reshape(2, step // 2, width).transpose(1, 0, 2)
    packed = jnp.concatenate(
        [
            down_part.reshape(8, layers * step // 8, rank),
            up_part,
            comp_part.reshape(8, step // 16, 2 * width),
        ],
        axis=1,
    )
    gathered = lax.all_gather(packed, "shard", axis=0)
    over_rows = lax.all_gather(over_weight, "shard", axis=1, tiled=True)
    small = samples // towers
    blocks = pooled[0].reshape(shards, towers, small, slot_most, emb).transpose(0, 3, 1, 2, 4)
    received = []
    for first, count in ((0, 16), (16, small - 16)):
        block = blocks[:, :, :, first : first + count].reshape(
            shards, slot_most, towers * count, emb
        )
        block = after(block, gathered if received else over_rows)
        received.append(
            lax.all_to_all(block, "shard", 0, 0, tiled=True).reshape(
                shards * slot_most, towers * count, emb
            )
        )
    slots = slot_order(table_tower, table_owner, tower_id, features // emb, slot_most)

    bias, squeeze_bias = cross_bias[0].astype(F32), comp_bias.astype(F32)
    totals = []
    for part in received:
        partial = tower_product(slots, part, gathered, bias, squeeze_bias, over_rows)
        pieces = partial.reshape(towers, part.shape[1] // towers, outputs)
        if totals:
            summed = lax.all_to_all(pieces, "tower", 0, 0, tiled=True).astype(F32)
            totals.append(jnp.sum(summed, axis=0))
        else:
            total = at(pieces, tower_id).astype(F32)
            for k in range(1, 16):
                moves = [(i, (i + k) % 16) for i in range(16)]
                piece = lax.ppermute(at(pieces, (tower_id + k) % 16), "tower", moves)
                total = total + piece.astype(F32)
            totals.append(total)
    total = jnp.concatenate(totals) + over_bias.astype(F32)
    return jax.nn.relu(total).astype(BF16)[None]


def solution(mesh):
    placed = (
        P("tower", None, "shard", None),
        P("tower", None, "shard", None),
        P("tower", None, None, "shard"),
        P("tower", None, None),
        P("tower", "shard", None),
        P("tower", None),
        P("tower", "shard"),
        P(),
        P(),
        P(),
    )
    return jax.shard_map(
        on_device, mesh=mesh, in_specs=placed, out_specs=P("shard", "tower", None), check_vma=False
    )
```

```python
import jax
import jax.numpy as jnp
from jax import lax
from jax.experimental import pallas as pl
from jax.experimental.pallas import tpu as pltpu
from jax.sharding import PartitionSpec as P

F32 = jnp.float32
BF16 = jnp.bfloat16


def slot_order(table_tower, table_owner, tower_id, per_tower, slot_most):
    table_count = table_tower.shape[0]
    index = jnp.arange(table_count, dtype=jnp.int32)
    inside = table_tower == tower_id
    earlier = index[None, :] < index[:, None]
    before = inside[None, :] & earlier
    position_in = jnp.sum(before.astype(jnp.int32), axis=1)
    same_owner = table_owner[None, :] == table_owner[:, None]
    own_slot = jnp.sum((before & same_owner).astype(jnp.int32), axis=1)
    wanted = table_owner * slot_most + own_slot
    picked = inside[None, :] & (
        position_in[None, :] == jnp.arange(per_tower, dtype=jnp.int32)[:, None]
    )
    return jnp.sum(jnp.where(picked, wanted[None, :], 0), axis=1)


QUARTERS = 4


def lower_kernel(slots, received, gathered, base, lowered, down, sems):
    features, rank = base.shape[1], lowered.shape[1]
    copy = pltpu.make_async_copy(gathered.at[:, pl.ds(0, down.shape[1]), :], down, sems.at[1])
    for p in range(features // 128):
        pltpu.make_async_copy(
            received.at[slots[p]], base.at[:, pl.ds(p * 128, 128)], sems.at[0]
        ).start()
    copy.start()
    pltpu.make_async_copy(base, base, sems.at[0]).wait()
    copy.wait()
    lowered[...] = jnp.dot(
        base[...], down.reshape(features, rank)[...], preferred_element_type=F32
    ).astype(BF16)


def raise_kernel(
    tables, lowered_first, gathered, rest, bias, comp_bias, out, base, state, up0, up1, down, comp, over, sems
):
    features = base.shape[1]
    shards, rank, step = up0.shape
    width, block = comp.shape[2], shards // QUARTERS
    first = []
    for q in range(QUARTERS):
        here, there = pl.ds(q * block * step, block * step), pl.ds(q * block, block)
        first.append(
            (
                pltpu.make_async_copy(tables.at[:, here], base.at[:, here], sems.at[2 * q]),
                pltpu.make_async_copy(
                    rest.at[there, pl.ds(0, rank), :], up0.at[there], sems.at[2 * q + 1]
                ),
            )
        )
    later = [
        pltpu.make_async_copy(source, target, sems.at[2 * QUARTERS + n])
        for n, (source, target) in enumerate(
            (
                (gathered.at[:, pl.ds(step, step), :], down),
                (rest.at[:, pl.ds(rank, rank), :], up1),
                (rest.at[:, pl.ds(2 * rank, step), :], comp),
                (rest.at[:, pl.ds(2 * rank + step, over.shape[1]), :], over),
            )
        )
    ]
    for pair in first:
        pair[0].start()
        pair[1].start()
    for copy in later:
        copy.start()

    lowered = lowered_first[...]
    for s in range(shards):
        if s % block == 0:
            first[s // block][0].wait()
            first[s // block][1].wait()
        here = pl.ds(s * step, step)
        raised = jnp.dot(lowered, up0[s], preferred_element_type=F32)
        part = base[:, here].astype(F32)
        state[:, here] = (part * (raised + bias[0:1, here]) + part).astype(BF16)
    later[0].wait()
    lowered = jnp.dot(
        state[...], down.reshape(features, rank)[...], preferred_element_type=F32
    ).astype(BF16)
    later[1].wait()
    for s in range(shards):
        here = pl.ds(s * step, step)
        raised = jnp.dot(lowered, up1[s], preferred_element_type=F32)
        part, held = base[:, here].astype(F32), state[:, here].astype(F32)
        state[:, here] = (part * (raised + bias[1:2, here]) + held).astype(BF16)
    later[2].wait()
    squeezed = jnp.dot(state[...], comp.reshape(features, width)[...], preferred_element_type=F32)
    squeezed = (squeezed + comp_bias[...]).astype(BF16)
    later[3].wait()
    over_t = over.reshape(over.shape[0] * over.shape[1], width)[...]
    out[...] = lax.dot_general(
        squeezed, over_t, (((1,), (1,)), ((), ())), preferred_element_type=F32
    ).astype(BF16)


def on_device(
    pooled,
    cross_down,
    cross_up,
    cross_bias,
    comp_weight,
    comp_bias,
    over_weight,
    over_bias,
    table_tower,
    table_owner,
):
    tower_id = lax.axis_index("tower")
    shards, towers = lax.axis_size("shard"), lax.axis_size("tower")
    _, batch, slot_most, emb = pooled.shape
    layers, rank, step = cross_up.shape[1:]
    features = step * shards
    width = comp_weight.shape[2]
    samples = batch // shards
    columns = over_weight.shape[1]
    outputs = columns * shards

    gathered = lax.all_gather(cross_down[0].reshape(layers * step, rank), "shard", axis=0)
    packed = jnp.concatenate(
        [cross_up[0].reshape(layers * rank, step), comp_weight[0], over_weight.T]
    )
    rest = lax.all_gather(packed, "shard", axis=0)
    by_slot = pooled[0].transpose(1, 0, 2).reshape(slot_most, shards, samples, emb)
    received = lax.all_to_all(
        by_slot.transpose(1, 0, 2, 3), "shard", split_axis=0, concat_axis=0, tiled=True
    ).reshape(shards * slot_most, samples, emb)
    slots = slot_order(table_tower, table_owner, tower_id, features // emb, slot_most)

    anywhere = pl.BlockSpec(memory_space=pl.ANY)

    def whole(*shape):
        return pl.BlockSpec(shape, lambda i, *_: (0,) * len(shape))

    tables, lowered = pl.pallas_call(
        lower_kernel,
        grid_spec=pltpu.PrefetchScalarGridSpec(
            num_scalar_prefetch=1,
            grid=(1,),
            in_specs=[anywhere, anywhere],
            out_specs=[whole(samples, features), whole(samples, rank)],
            scratch_shapes=[
                pltpu.VMEM((shards, step, rank), BF16),
                pltpu.SemaphoreType.DMA((2,)),
            ],
        ),
        out_shape=[
            jax.ShapeDtypeStruct((samples, features), BF16),
            jax.ShapeDtypeStruct((samples, rank), BF16),
        ],
        compiler_params=pltpu.CompilerParams(vmem_limit_bytes=32 * 2**20),
        cost_estimate=pl.CostEstimate(
            flops=2 * samples * features * rank, bytes_accessed=12 * 10**6, transcendentals=0
        ),
    )(slots, received, gathered)

    partial = pl.pallas_call(
        raise_kernel,
        grid=(1,),
        in_specs=[
            anywhere,
            whole(samples, rank),
            anywhere,
            anywhere,
            whole(layers, features),
            whole(1, width),
        ],
        out_specs=whole(samples, outputs),
        scratch_shapes=[
            pltpu.VMEM((samples, features), BF16),
            pltpu.VMEM((samples, features), BF16),
            pltpu.VMEM((shards, rank, step), BF16),
            pltpu.VMEM((shards, rank, step), BF16),
            pltpu.VMEM((shards, step, rank), BF16),
            pltpu.VMEM((shards, step, width), BF16),
            pltpu.VMEM((shards, columns, width), BF16),
            pltpu.SemaphoreType.DMA((2 * QUARTERS + 4,)),
        ],
        out_shape=jax.ShapeDtypeStruct((samples, outputs), BF16),
        compiler_params=pltpu.CompilerParams(vmem_limit_bytes=48 * 2**20),
        cost_estimate=pl.CostEstimate(flops=6 * 10**9, bytes_accessed=20 * 10**6, transcendentals=0),
    )(tables, lowered, gathered, rest, cross_bias[0].astype(F32), comp_bias.astype(F32))

    summed = lax.all_to_all(
        partial.reshape(towers, samples // towers, outputs), "tower", 0, 0, tiled=True
    )
    total = jnp.sum(summed.astype(F32), axis=0) + over_bias.astype(F32)
    return jax.nn.relu(total).astype(BF16)[None]


def solution(mesh):
    placed = (
        P("tower", None, "shard", None),
        P("tower", None, "shard", None),
        P("tower", None, None, "shard"),
        P("tower", None, None),
        P("tower", "shard", None),
        P("tower", None),
        P("tower", "shard"),
        P(),
        P(),
        P(),
    )
    return jax.shard_map(
        on_device, mesh=mesh, in_specs=placed, out_specs=P("shard", "tower", None), check_vma=False
    )
```

```python
import jax
import jax.numpy as jnp
from jax import lax
from jax.experimental import pallas as pl
from jax.experimental.pallas import tpu as pltpu
from jax.sharding import PartitionSpec as P

F32 = jnp.float32
BF16 = jnp.bfloat16


def slot_order(table_tower, table_owner, tower_id, per_tower, slot_most):
    table_count = table_tower.shape[0]
    index = jnp.arange(table_count, dtype=jnp.int32)
    inside = table_tower == tower_id
    earlier = index[None, :] < index[:, None]
    before = inside[None, :] & earlier
    position_in = jnp.sum(before.astype(jnp.int32), axis=1)
    same_owner = table_owner[None, :] == table_owner[:, None]
    own_slot = jnp.sum((before & same_owner).astype(jnp.int32), axis=1)
    wanted = table_owner * slot_most + own_slot
    picked = inside[None, :] & (
        position_in[None, :] == jnp.arange(per_tower, dtype=jnp.int32)[:, None]
    )
    return jnp.sum(jnp.where(picked, wanted[None, :], 0), axis=1)


QUARTERS = 4
BACK = (0, 1, 15, 2, 14, 3, 13, 4, 12, 5, 11, 6, 10, 7, 9, 8)


def tower_kernel(places, *refs):
    pieces, refs = refs[:-13], refs[-13:]
    weights, bias, comp_bias, out, base, state, down0, down1, up0, up1, comp, over, sems = refs
    features = base.shape[1]
    shards, step, rank = down0.shape
    width, slot_most = comp.shape[2], pieces[0].shape[0]
    block, half = shards // QUARTERS, rank // 2
    me = places[shards * slot_most]
    for k in range(shards):
        owner = lax.rem(me + shards - BACK[k], shards)
        for slot in range(slot_most):
            place = places[owner * slot_most + slot]

            @pl.when(place >= 0)
            def _(k=k, slot=slot, place=place):
                pltpu.make_async_copy(
                    pieces[k].at[slot],
                    base.at[:, pl.ds(pl.multiple_of(place * 128, 128), 128)],
                    sems.at[0],
                ).start()

    def bring(first, count, target, n):
        return pltpu.make_async_copy(weights.at[:, pl.ds(first, count), :], target, sems.at[n])

    early = []
    for q in range(QUARTERS):
        there = pl.ds(q * block, block)
        for h in range(2):
            early.append(
                pltpu.make_async_copy(
                    weights.at[there, pl.ds(2 * step * h, step), :],
                    down0.at[there, :, pl.ds(h * half, half)],
                    sems.at[1 + 2 * q + h],
                )
            )
    n, at_up = 1 + 2 * QUARTERS, 4 * step
    bring_up0 = bring(at_up, rank, up0, n)
    bring_down1 = [
        bring(2 * step * h + step, step, down1.at[:, :, pl.ds(h * half, half)], n + 1 + h)
        for h in range(2)
    ]
    bring_up1 = bring(at_up + rank, rank, up1, n + 3)
    bring_comp = bring(at_up + 2 * rank, step, comp, n + 4)
    bring_over = bring(at_up + 2 * rank + step, over.shape[1], over, n + 5)
    for copy in (*early, bring_up0, *bring_down1, bring_up1, bring_comp, bring_over):
        copy.start()

    pltpu.make_async_copy(base, base, sems.at[0]).wait()
    total = None
    for q in range(QUARTERS):
        early[2 * q].wait()
        early[2 * q + 1].wait()
        deep = block * step
        part = jnp.dot(
            base[:, pl.ds(q * deep, deep)],
            down0.reshape(features, rank)[pl.ds(q * deep, deep), :],
            preferred_element_type=F32,
        )
        total = part if total is None else total + part
    lowered = total.astype(BF16)
    bring_up0.wait()
    for s in range(shards):
        here = pl.ds(s * step, step)
        raised = jnp.dot(lowered, up0[s], preferred_element_type=F32)
        part = base[:, here].astype(F32)
        state[:, here] = (part * (raised + bias[0:1, here]) + part).astype(BF16)
    bring_down1[0].wait()
    bring_down1[1].wait()
    lowered = jnp.dot(
        state[...], down1.reshape(features, rank)[...], preferred_element_type=F32
    ).astype(BF16)
    bring_up1.wait()
    for s in range(shards):
        here = pl.ds(s * step, step)
        raised = jnp.dot(lowered, up1[s], preferred_element_type=F32)
        part, held = base[:, here].astype(F32), state[:, here].astype(F32)
        state[:, here] = (part * (raised + bias[1:2, here]) + held).astype(BF16)
    bring_comp.wait()
    squeezed = jnp.dot(state[...], comp.reshape(features, width)[...], preferred_element_type=F32)
    squeezed = (squeezed + comp_bias[...]).astype(BF16)
    bring_over.wait()
    over_t = over.reshape(over.shape[0] * over.shape[1], width)[...]
    out[...] = lax.dot_general(
        squeezed, over_t, (((1,), (1,)), ((), ())), preferred_element_type=F32
    ).astype(BF16)


def on_device(
    pooled,
    cross_down,
    cross_up,
    cross_bias,
    comp_weight,
    comp_bias,
    over_weight,
    over_bias,
    table_tower,
    table_owner,
):
    tower_id, shard = lax.axis_index("tower"), lax.axis_index("shard")
    shards, towers = 16, 16
    _, batch, slot_most, emb = pooled.shape
    layers, rank, step = cross_up.shape[1:]
    features = step * shards
    width = comp_weight.shape[2]
    samples = batch // shards
    columns = over_weight.shape[1]
    outputs = columns * shards

    down = cross_down[0].reshape(layers * step, rank)
    packed = jnp.concatenate(
        [
            down[:, : rank // 2],
            down[:, rank // 2 :],
            cross_up[0].reshape(layers * rank, step),
            comp_weight[0],
            over_weight.T,
        ]
    )
    weights = lax.all_gather(packed, "shard", axis=0)

    by_slot = pooled[0].transpose(1, 0, 2).reshape(slot_most, shards, samples, emb)

    def piece_for(to):
        return lax.dynamic_index_in_dim(by_slot, to % 16, 1, keepdims=False)

    pieces = [piece_for(shard)]
    for k in BACK[1:]:
        moves = [(i, (i + k) % 16) for i in range(16)]
        pieces.append(lax.ppermute(piece_for(shard + k), "shard", moves))

    slots = slot_order(table_tower, table_owner, tower_id, features // emb, slot_most)
    index = jnp.arange(shards * slot_most, dtype=jnp.int32)[:, None]
    turn = jnp.arange(1, slots.shape[0] + 1, dtype=jnp.int32)[None, :]
    places = jnp.sum(jnp.where(slots[None, :] == index, turn, 0), axis=1) - 1
    places = jnp.concatenate([places, shard[None]]).astype(jnp.int32)

    anywhere = pl.BlockSpec(memory_space=pl.ANY)

    def whole(*shape):
        return pl.BlockSpec(shape, lambda i, *_: (0,) * len(shape))

    partial = pl.pallas_call(
        tower_kernel,
        grid_spec=pltpu.PrefetchScalarGridSpec(
            num_scalar_prefetch=1,
            grid=(1,),
            in_specs=[anywhere] * (shards + 1) + [whole(layers, features), whole(1, width)],
            out_specs=whole(samples, outputs),
            scratch_shapes=[
                pltpu.VMEM((samples, features), BF16),
                pltpu.VMEM((samples, features), BF16),
                pltpu.VMEM((shards, step, rank), BF16),
                pltpu.VMEM((shards, step, rank), BF16),
                pltpu.VMEM((shards, rank, step), BF16),
                pltpu.VMEM((shards, rank, step), BF16),
                pltpu.VMEM((shards, step, width), BF16),
                pltpu.VMEM((shards, columns, width), BF16),
                pltpu.SemaphoreType.DMA((7 + 2 * QUARTERS,)),
            ],
        ),
        out_shape=jax.ShapeDtypeStruct((samples, outputs), BF16),
        compiler_params=pltpu.CompilerParams(vmem_limit_bytes=48 * 2**20),
        cost_estimate=pl.CostEstimate(flops=8 * 10**9, bytes_accessed=24 * 10**6, transcendentals=0),
    )(
        places,
        *pieces,
        weights,
        cross_bias[0].astype(F32),
        comp_bias.astype(F32),
    )

    summed = lax.all_to_all(
        partial.reshape(towers, samples // towers, outputs), "tower", 0, 0, tiled=True
    )
    total = jnp.sum(summed.astype(F32), axis=0) + over_bias.astype(F32)
    return jax.nn.relu(total).astype(BF16)[None]


def solution(mesh):
    placed = (
        P("tower", None, "shard", None),
        P("tower", None, "shard", None),
        P("tower", None, None, "shard"),
        P("tower", None, None),
        P("tower", "shard", None),
        P("tower", None),
        P("tower", "shard"),
        P(),
        P(),
        P(),
    )
    return jax.shard_map(
        on_device, mesh=mesh, in_specs=placed, out_specs=P("shard", "tower", None), check_vma=False
    )
```

```python
import jax
import jax.numpy as jnp
from jax import lax
from jax.experimental import pallas as pl
from jax.experimental.pallas import tpu as pltpu
from jax.sharding import PartitionSpec as P

F32 = jnp.float32
BF16 = jnp.bfloat16


def slot_order(table_tower, table_owner, tower_id, per_tower, slot_most):
    table_count = table_tower.shape[0]
    index = jnp.arange(table_count, dtype=jnp.int32)
    inside = table_tower == tower_id
    earlier = index[None, :] < index[:, None]
    before = inside[None, :] & earlier
    position_in = jnp.sum(before.astype(jnp.int32), axis=1)
    same_owner = table_owner[None, :] == table_owner[:, None]
    own_slot = jnp.sum((before & same_owner).astype(jnp.int32), axis=1)
    wanted = table_owner * slot_most + own_slot
    picked = inside[None, :] & (
        position_in[None, :] == jnp.arange(per_tower, dtype=jnp.int32)[:, None]
    )
    return jnp.sum(jnp.where(picked, wanted[None, :], 0), axis=1)


QUARTERS = 4
BACK = (0, 1, 15, 2, 14, 3, 13, 4, 12, 5, 11, 6, 10, 7, 9, 8)


def table_kernel(places, *refs):
    pieces, (base, sem) = refs[:-2], refs[-2:]
    shards, slot_most = len(pieces), pieces[0].shape[0]
    me = places[shards * slot_most]
    for k in range(shards):
        owner = lax.rem(me + shards - BACK[k], shards)
        for slot in range(slot_most):
            place = places[owner * slot_most + slot]

            @pl.when(place >= 0)
            def _(k=k, slot=slot, place=place):
                pltpu.make_async_copy(
                    pieces[k].at[slot],
                    base.at[:, pl.ds(pl.multiple_of(place * 128, 128), 128)],
                    sem,
                ).start()

    pltpu.make_async_copy(base, base, sem).wait()


def tower_kernel(
    tables, weights, bias, comp_bias, out, base, state, down0, down1, up0, up1, comp, over, sems
):
    features = base.shape[1]
    shards, step, rank = down0.shape
    width = comp.shape[2]
    block, half = shards // QUARTERS, rank // 2

    def bring(first, count, target, n):
        return pltpu.make_async_copy(weights.at[:, pl.ds(first, count), :], target, sems.at[n])

    early = []
    for q in range(QUARTERS):
        there, columns = pl.ds(q * block, block), pl.ds(q * block * step, block * step)
        early.append(
            pltpu.make_async_copy(tables.at[:, columns], base.at[:, columns], sems.at[3 * q])
        )
        for h in range(2):
            early.append(
                pltpu.make_async_copy(
                    weights.at[there, pl.ds(2 * step * h, step), :],
                    down0.at[there, :, pl.ds(h * half, half)],
                    sems.at[3 * q + 1 + h],
                )
            )
    n, at_up = 3 * QUARTERS, 4 * step
    bring_up0 = bring(at_up, rank, up0, n)
    bring_down1 = [
        bring(2 * step * h + step, step, down1.at[:, :, pl.ds(h * half, half)], n + 1 + h)
        for h in range(2)
    ]
    bring_up1 = bring(at_up + rank, rank, up1, n + 3)
    bring_comp = bring(at_up + 2 * rank, step, comp, n + 4)
    bring_over = bring(at_up + 2 * rank + step, over.shape[1], over, n + 5)
    for copy in (*early, bring_up0, *bring_down1, bring_up1, bring_comp, bring_over):
        copy.start()

    total = None
    for q in range(QUARTERS):
        for copy in early[3 * q : 3 * q + 3]:
            copy.wait()
        deep = block * step
        part = jnp.dot(
            base[:, pl.ds(q * deep, deep)],
            down0.reshape(features, rank)[pl.ds(q * deep, deep), :],
            preferred_element_type=F32,
        )
        total = part if total is None else total + part
    lowered = total.astype(BF16)
    bring_up0.wait()
    for s in range(shards):
        here = pl.ds(s * step, step)
        raised = jnp.dot(lowered, up0[s], preferred_element_type=F32)
        part = base[:, here].astype(F32)
        state[:, here] = (part * (raised + bias[0:1, here]) + part).astype(BF16)
    bring_down1[0].wait()
    bring_down1[1].wait()
    lowered = jnp.dot(
        state[...], down1.reshape(features, rank)[...], preferred_element_type=F32
    ).astype(BF16)
    bring_up1.wait()
    for s in range(shards):
        here = pl.ds(s * step, step)
        raised = jnp.dot(lowered, up1[s], preferred_element_type=F32)
        part, held = base[:, here].astype(F32), state[:, here].astype(F32)
        state[:, here] = (part * (raised + bias[1:2, here]) + held).astype(BF16)
    bring_comp.wait()
    squeezed = jnp.dot(state[...], comp.reshape(features, width)[...], preferred_element_type=F32)
    squeezed = (squeezed + comp_bias[...]).astype(BF16)
    bring_over.wait()
    over_t = over.reshape(over.shape[0] * over.shape[1], width)[...]
    out[...] = lax.dot_general(
        squeezed, over_t, (((1,), (1,)), ((), ())), preferred_element_type=F32
    ).astype(BF16)


def on_device(
    pooled,
    cross_down,
    cross_up,
    cross_bias,
    comp_weight,
    comp_bias,
    over_weight,
    over_bias,
    table_tower,
    table_owner,
):
    tower_id, shard = lax.axis_index("tower"), lax.axis_index("shard")
    shards, towers = 16, 16
    _, batch, slot_most, emb = pooled.shape
    layers, rank, step = cross_up.shape[1:]
    features = step * shards
    width = comp_weight.shape[2]
    samples = batch // shards
    columns = over_weight.shape[1]
    outputs = columns * shards

    down = cross_down[0].reshape(layers * step, rank)
    packed = jnp.concatenate(
        [
            down[:, : rank // 2],
            down[:, rank // 2 :],
            cross_up[0].reshape(layers * rank, step),
            comp_weight[0],
            over_weight.T,
        ]
    )
    weights = lax.all_gather(packed, "shard", axis=0)

    by_slot = pooled[0].transpose(1, 0, 2).reshape(slot_most, shards, samples, emb)

    def piece_for(to):
        return lax.dynamic_index_in_dim(by_slot, to % 16, 1, keepdims=False)

    pieces = [piece_for(shard)]
    for k in BACK[1:]:
        moves = [(i, (i + k) % 16) for i in range(16)]
        pieces.append(lax.ppermute(piece_for(shard + k), "shard", moves))

    slots = slot_order(table_tower, table_owner, tower_id, features // emb, slot_most)
    index = jnp.arange(shards * slot_most, dtype=jnp.int32)[:, None]
    turn = jnp.arange(1, slots.shape[0] + 1, dtype=jnp.int32)[None, :]
    places = jnp.sum(jnp.where(slots[None, :] == index, turn, 0), axis=1) - 1
    places = jnp.concatenate([places, shard[None]]).astype(jnp.int32)

    anywhere = pl.BlockSpec(memory_space=pl.ANY)

    def whole(*shape):
        return pl.BlockSpec(shape, lambda i, *_: (0,) * len(shape))

    tables = pl.pallas_call(
        table_kernel,
        grid_spec=pltpu.PrefetchScalarGridSpec(
            num_scalar_prefetch=1,
            grid=(1,),
            in_specs=[anywhere] * shards,
            out_specs=whole(samples, features),
            scratch_shapes=[pltpu.SemaphoreType.DMA],
        ),
        out_shape=jax.ShapeDtypeStruct((samples, features), BF16),
        compiler_params=pltpu.CompilerParams(vmem_limit_bytes=12 * 2**20),
        cost_estimate=pl.CostEstimate(flops=0, bytes_accessed=10 * 10**6, transcendentals=0),
    )(places, *pieces)

    partial = pl.pallas_call(
        tower_kernel,
        grid_spec=pl.GridSpec(
            grid=(1,),
            in_specs=[anywhere, anywhere, whole(layers, features), whole(1, width)],
            out_specs=whole(samples, outputs),
            scratch_shapes=[
                pltpu.VMEM((samples, features), BF16),
                pltpu.VMEM((samples, features), BF16),
                pltpu.VMEM((shards, step, rank), BF16),
                pltpu.VMEM((shards, step, rank), BF16),
                pltpu.VMEM((shards, rank, step), BF16),
                pltpu.VMEM((shards, rank, step), BF16),
                pltpu.VMEM((shards, step, width), BF16),
                pltpu.VMEM((shards, columns, width), BF16),
                pltpu.SemaphoreType.DMA((6 + 3 * QUARTERS,)),
            ],
        ),
        out_shape=jax.ShapeDtypeStruct((samples, outputs), BF16),
        compiler_params=pltpu.CompilerParams(vmem_limit_bytes=36 * 2**20),
        cost_estimate=pl.CostEstimate(flops=8 * 10**9, bytes_accessed=24 * 10**6, transcendentals=0),
    )(tables, weights, cross_bias[0].astype(F32), comp_bias.astype(F32))

    summed = lax.all_to_all(
        partial.reshape(towers, samples // towers, outputs), "tower", 0, 0, tiled=True
    )
    total = jnp.sum(summed.astype(F32), axis=0) + over_bias.astype(F32)
    return jax.nn.relu(total).astype(BF16)[None]


def solution(mesh):
    placed = (
        P("tower", None, "shard", None),
        P("tower", None, "shard", None),
        P("tower", None, None, "shard"),
        P("tower", None, None),
        P("tower", "shard", None),
        P("tower", None),
        P("tower", "shard"),
        P(),
        P(),
        P(),
    )
    return jax.shard_map(
        on_device, mesh=mesh, in_specs=placed, out_specs=P("shard", "tower", None), check_vma=False
    )
```

```python
import jax
import jax.numpy as jnp
from jax import lax
from jax.experimental import pallas as pl
from jax.experimental.pallas import tpu as pltpu
from jax.sharding import PartitionSpec as P

F32 = jnp.float32
BF16 = jnp.bfloat16


def slot_order(table_tower, table_owner, tower_id, per_tower, slot_most):
    table_count = table_tower.shape[0]
    index = jnp.arange(table_count, dtype=jnp.int32)
    inside = table_tower == tower_id
    earlier = index[None, :] < index[:, None]
    before = inside[None, :] & earlier
    position_in = jnp.sum(before.astype(jnp.int32), axis=1)
    same_owner = table_owner[None, :] == table_owner[:, None]
    own_slot = jnp.sum((before & same_owner).astype(jnp.int32), axis=1)
    wanted = table_owner * slot_most + own_slot
    picked = inside[None, :] & (
        position_in[None, :] == jnp.arange(per_tower, dtype=jnp.int32)[:, None]
    )
    return jnp.sum(jnp.where(picked, wanted[None, :], 0), axis=1)


QUARTERS = 4
BACK = (0, 1, 15, 2, 14, 3, 13, 4, 12, 5, 11, 6, 10, 7, 9, 8)


def pack_kernel(down, up, comp, over, out, sems):
    half = out.shape[1]
    sources = [down.at[:, pl.ds(0, half)], down.at[:, pl.ds(half, half)], up, comp, over]
    copies, first = [], 0
    for n, source in enumerate(sources):
        count = source.shape[0]
        copies.append(pltpu.make_async_copy(source, out.at[pl.ds(first, count), :], sems.at[n]))
        first += count
    for copy in copies:
        copy.start()
    for copy in copies:
        copy.wait()


def table_kernel(places, *refs):
    pieces, (base, sem) = refs[:-2], refs[-2:]
    shards, slot_most = len(pieces), pieces[0].shape[0]
    me = places[shards * slot_most]
    for k in range(shards):
        owner = lax.rem(me + shards - BACK[k], shards)
        for slot in range(slot_most):
            place = places[owner * slot_most + slot]

            @pl.when(place >= 0)
            def _(k=k, slot=slot, place=place):
                pltpu.make_async_copy(
                    pieces[k].at[slot],
                    base.at[:, pl.ds(pl.multiple_of(place * 128, 128), 128)],
                    sem,
                ).start()

    pltpu.make_async_copy(base, base, sem).wait()


def tower_kernel(
    tables, weights, bias, comp_bias, out, base, state, down0, down1, up0, up1, comp, over, sems
):
    features = base.shape[1]
    shards, step, rank = down0.shape
    width = comp.shape[2]
    block, half = shards // QUARTERS, rank // 2

    def bring(first, count, target, n):
        return pltpu.make_async_copy(weights.at[:, pl.ds(first, count), :], target, sems.at[n])

    early = []
    for q in range(QUARTERS):
        there, columns = pl.ds(q * block, block), pl.ds(q * block * step, block * step)
        early.append(
            pltpu.make_async_copy(tables.at[:, columns], base.at[:, columns], sems.at[3 * q])
        )
        for h in range(2):
            early.append(
                pltpu.make_async_copy(
                    weights.at[there, pl.ds(2 * step * h, step), :],
                    down0.at[there, :, pl.ds(h * half, half)],
                    sems.at[3 * q + 1 + h],
                )
            )
    n, at_up = 3 * QUARTERS, 4 * step
    bring_up0 = bring(at_up, rank, up0, n)
    bring_down1 = [
        bring(2 * step * h + step, step, down1.at[:, :, pl.ds(h * half, half)], n + 1 + h)
        for h in range(2)
    ]
    bring_up1 = bring(at_up + rank, rank, up1, n + 3)
    bring_comp = bring(at_up + 2 * rank, step, comp, n + 4)
    bring_over = bring(at_up + 2 * rank + step, over.shape[1], over, n + 5)
    for copy in (*early, bring_up0, *bring_down1, bring_up1, bring_comp, bring_over):
        copy.start()

    total = None
    for q in range(QUARTERS):
        for copy in early[3 * q : 3 * q + 3]:
            copy.wait()
        deep = block * step
        part = jnp.dot(
            base[:, pl.ds(q * deep, deep)],
            down0.reshape(features, rank)[pl.ds(q * deep, deep), :],
            preferred_element_type=F32,
        )
        total = part if total is None else total + part
    lowered = total.astype(BF16)
    bring_up0.wait()
    for s in range(shards):
        here = pl.ds(s * step, step)
        raised = jnp.dot(lowered, up0[s], preferred_element_type=F32)
        part = base[:, here].astype(F32)
        state[:, here] = (part * (raised + bias[0:1, here]) + part).astype(BF16)
    bring_down1[0].wait()
    bring_down1[1].wait()
    lowered = jnp.dot(
        state[...], down1.reshape(features, rank)[...], preferred_element_type=F32
    ).astype(BF16)
    bring_up1.wait()
    for s in range(shards):
        here = pl.ds(s * step, step)
        raised = jnp.dot(lowered, up1[s], preferred_element_type=F32)
        part, held = base[:, here].astype(F32), state[:, here].astype(F32)
        state[:, here] = (part * (raised + bias[1:2, here]) + held).astype(BF16)
    bring_comp.wait()
    squeezed = jnp.dot(state[...], comp.reshape(features, width)[...], preferred_element_type=F32)
    squeezed = (squeezed + comp_bias[...]).astype(BF16)
    bring_over.wait()
    over_t = over.reshape(over.shape[0] * over.shape[1], width)[...]
    out[...] = lax.dot_general(
        squeezed, over_t, (((1,), (1,)), ((), ())), preferred_element_type=F32
    ).astype(BF16)


def on_device(
    pooled,
    cross_down,
    cross_up,
    cross_bias,
    comp_weight,
    comp_bias,
    over_weight,
    over_bias,
    table_tower,
    table_owner,
):
    tower_id, shard = lax.axis_index("tower"), lax.axis_index("shard")
    shards, towers = 16, 16
    _, batch, slot_most, emb = pooled.shape
    layers, rank, step = cross_up.shape[1:]
    features = step * shards
    width = comp_weight.shape[2]
    samples = batch // shards
    columns = over_weight.shape[1]
    outputs = columns * shards

    parts = (
        cross_down[0].reshape(layers * step, rank),
        cross_up[0].reshape(layers * rank, step),
        comp_weight[0],
        over_weight.T,
    )
    packed = pl.pallas_call(
        pack_kernel,
        in_specs=[pl.BlockSpec(memory_space=pl.ANY)] * len(parts),
        out_specs=pl.BlockSpec(memory_space=pl.ANY),
        scratch_shapes=[pltpu.SemaphoreType.DMA((len(parts) + 1,))],
        out_shape=jax.ShapeDtypeStruct((sum(p.size for p in parts) // step, step), BF16),
        compiler_params=pltpu.CompilerParams(vmem_limit_bytes=58 * 2**20),
    )(*parts)
    weights = lax.all_gather(packed, "shard", axis=0)

    by_slot = pooled[0].transpose(1, 0, 2).reshape(slot_most, shards, samples, emb)

    def piece_for(to):
        return lax.dynamic_index_in_dim(by_slot, to % 16, 1, keepdims=False)

    pieces = [piece_for(shard)]
    for k in BACK[1:]:
        moves = [(i, (i + k) % 16) for i in range(16)]
        pieces.append(lax.ppermute(piece_for(shard + k), "shard", moves))

    slots = slot_order(table_tower, table_owner, tower_id, features // emb, slot_most)
    index = jnp.arange(shards * slot_most, dtype=jnp.int32)[:, None]
    turn = jnp.arange(1, slots.shape[0] + 1, dtype=jnp.int32)[None, :]
    places = jnp.sum(jnp.where(slots[None, :] == index, turn, 0), axis=1) - 1
    places = jnp.concatenate([places, shard[None]]).astype(jnp.int32)

    anywhere = pl.BlockSpec(memory_space=pl.ANY)

    def whole(*shape):
        return pl.BlockSpec(shape, lambda i, *_: (0,) * len(shape))

    tables = pl.pallas_call(
        table_kernel,
        grid_spec=pltpu.PrefetchScalarGridSpec(
            num_scalar_prefetch=1,
            grid=(1,),
            in_specs=[anywhere] * shards,
            out_specs=whole(samples, features),
            scratch_shapes=[pltpu.SemaphoreType.DMA],
        ),
        out_shape=jax.ShapeDtypeStruct((samples, features), BF16),
        compiler_params=pltpu.CompilerParams(vmem_limit_bytes=12 * 2**20),
        cost_estimate=pl.CostEstimate(flops=0, bytes_accessed=10 * 10**6, transcendentals=0),
    )(places, *pieces)

    partial = pl.pallas_call(
        tower_kernel,
        grid_spec=pl.GridSpec(
            grid=(1,),
            in_specs=[anywhere, anywhere, whole(layers, features), whole(1, width)],
            out_specs=whole(samples, outputs),
            scratch_shapes=[
                pltpu.VMEM((samples, features), BF16),
                pltpu.VMEM((samples, features), BF16),
                pltpu.VMEM((shards, step, rank), BF16),
                pltpu.VMEM((shards, step, rank), BF16),
                pltpu.VMEM((shards, rank, step), BF16),
                pltpu.VMEM((shards, rank, step), BF16),
                pltpu.VMEM((shards, step, width), BF16),
                pltpu.VMEM((shards, columns, width), BF16),
                pltpu.SemaphoreType.DMA((6 + 3 * QUARTERS,)),
            ],
        ),
        out_shape=jax.ShapeDtypeStruct((samples, outputs), BF16),
        compiler_params=pltpu.CompilerParams(vmem_limit_bytes=58 * 2**20),
        cost_estimate=pl.CostEstimate(flops=8 * 10**9, bytes_accessed=24 * 10**6, transcendentals=0),
    )(tables, weights, cross_bias[0].astype(F32), comp_bias.astype(F32))

    summed = lax.all_to_all(
        partial.reshape(towers, samples // towers, outputs), "tower", 0, 0, tiled=True
    )
    total = jnp.sum(summed.astype(F32), axis=0) + over_bias.astype(F32)
    return jax.nn.relu(total).astype(BF16)[None]


def solution(mesh):
    placed = (
        P("tower", None, "shard", None),
        P("tower", None, "shard", None),
        P("tower", None, None, "shard"),
        P("tower", None, None),
        P("tower", "shard", None),
        P("tower", None),
        P("tower", "shard"),
        P(),
        P(),
        P(),
    )
    return jax.shard_map(
        on_device, mesh=mesh, in_specs=placed, out_specs=P("shard", "tower", None), check_vma=False
    )
```

```python
import jax
import jax.numpy as jnp
from jax import lax
from jax.experimental import pallas as pl
from jax.experimental.pallas import tpu as pltpu
from jax.sharding import PartitionSpec as P

F32 = jnp.float32
BF16 = jnp.bfloat16


def slot_order(table_tower, table_owner, tower_id, per_tower, slot_most):
    table_count = table_tower.shape[0]
    index = jnp.arange(table_count, dtype=jnp.int32)
    inside = table_tower == tower_id
    earlier = index[None, :] < index[:, None]
    before = inside[None, :] & earlier
    position_in = jnp.sum(before.astype(jnp.int32), axis=1)
    same_owner = table_owner[None, :] == table_owner[:, None]
    own_slot = jnp.sum((before & same_owner).astype(jnp.int32), axis=1)
    wanted = table_owner * slot_most + own_slot
    picked = inside[None, :] & (
        position_in[None, :] == jnp.arange(per_tower, dtype=jnp.int32)[:, None]
    )
    return jnp.sum(jnp.where(picked, wanted[None, :], 0), axis=1)


QUARTERS = 4
BACK = (0, 8, 1, 15, 7, 2, 14, 9, 3, 13, 6, 4, 12, 10, 5, 11)


def pack_kernel(down, up, comp, out, sems):
    half = out.shape[1]
    sources = [down.at[:, pl.ds(0, half)], down.at[:, pl.ds(half, half)], up, comp]
    copies, first = [], 0
    for n, source in enumerate(sources):
        count = source.shape[0]
        copies.append(pltpu.make_async_copy(source, out.at[pl.ds(first, count), :], sems.at[n]))
        first += count
    for copy in copies:
        copy.start()
    for copy in copies:
        copy.wait()


def table_kernel(places, *refs):
    pieces, (base, sem) = refs[:-2], refs[-2:]
    shards, slot_most = len(pieces), pieces[0].shape[0]
    me = places[shards * slot_most]
    for k in range(shards):
        owner = lax.rem(me + shards - BACK[k], shards)
        for slot in range(slot_most):
            place = places[owner * slot_most + slot]

            @pl.when(place >= 0)
            def _(k=k, slot=slot, place=place):
                pltpu.make_async_copy(
                    pieces[k].at[slot],
                    base.at[:, pl.ds(pl.multiple_of(place * 128, 128), 128)],
                    sem,
                ).start()

    pltpu.make_async_copy(base, base, sem).wait()


def tower_kernel(
    tables, weights, bias, comp_bias, out, base, state, down0, down1, up0, up1, comp, sems
):
    features = base.shape[1]
    shards, step, rank = down0.shape
    width = comp.shape[2]
    block, half = shards // QUARTERS, rank // 2

    def bring(first, count, target, n):
        return pltpu.make_async_copy(weights.at[:, pl.ds(first, count), :], target, sems.at[n])

    early = []
    for q in range(QUARTERS):
        there, columns = pl.ds(q * block, block), pl.ds(q * block * step, block * step)
        early.append(
            pltpu.make_async_copy(tables.at[:, columns], base.at[:, columns], sems.at[3 * q])
        )
        for h in range(2):
            early.append(
                pltpu.make_async_copy(
                    weights.at[there, pl.ds(2 * step * h, step), :],
                    down0.at[there, :, pl.ds(h * half, half)],
                    sems.at[3 * q + 1 + h],
                )
            )
    n, at_up = 3 * QUARTERS, 4 * step
    bring_up0 = bring(at_up, rank, up0, n)
    bring_down1 = [
        bring(2 * step * h + step, step, down1.at[:, :, pl.ds(h * half, half)], n + 1 + h)
        for h in range(2)
    ]
    bring_up1 = bring(at_up + rank, rank, up1, n + 3)
    bring_comp = bring(at_up + 2 * rank, step, comp, n + 4)
    for copy in (*early, bring_up0, *bring_down1, bring_up1, bring_comp):
        copy.start()

    total = None
    for q in range(QUARTERS):
        for copy in early[3 * q : 3 * q + 3]:
            copy.wait()
        deep = block * step
        part = jnp.dot(
            base[:, pl.ds(q * deep, deep)],
            down0.reshape(features, rank)[pl.ds(q * deep, deep), :],
            preferred_element_type=F32,
        )
        total = part if total is None else total + part
    lowered = total.astype(BF16)
    bring_up0.wait()
    for s in range(shards):
        here = pl.ds(s * step, step)
        raised = jnp.dot(lowered, up0[s], preferred_element_type=F32)
        part = base[:, here].astype(F32)
        state[:, here] = (part * (raised + bias[0:1, here]) + part).astype(BF16)
    bring_down1[0].wait()
    bring_down1[1].wait()
    lowered = jnp.dot(
        state[...], down1.reshape(features, rank)[...], preferred_element_type=F32
    ).astype(BF16)
    bring_up1.wait()
    for s in range(shards):
        here = pl.ds(s * step, step)
        raised = jnp.dot(lowered, up1[s], preferred_element_type=F32)
        part, held = base[:, here].astype(F32), state[:, here].astype(F32)
        state[:, here] = (part * (raised + bias[1:2, here]) + held).astype(BF16)
    bring_comp.wait()
    squeezed = jnp.dot(state[...], comp.reshape(features, width)[...], preferred_element_type=F32)
    out[...] = (squeezed + comp_bias[...]).astype(BF16)


def over_kernel(place, joined, *refs):
    pieces, (bias, out, held, sems) = refs[:-4], refs[-4:]
    copies = [
        pltpu.make_async_copy(piece, held.at[n], sems.at[n]) for n, piece in enumerate(pieces)
    ]
    for copy in copies:
        copy.start()
    x, y = place[0], place[1]
    total = None
    for n, copy in enumerate(copies):
        copy.wait()
        tower = 4 * lax.rem(x + 4 - n // 4, 4) + lax.rem(y + 4 - n % 4, 4)
        part = lax.dot_general(
            joined[tower], held[n], (((1,), (1,)), ((), ())), preferred_element_type=F32
        )
        total = part if total is None else total + part
    out[...] = jnp.maximum(total + bias[...], 0.0).astype(BF16)


def once(*others):
    zero = jnp.int32(0)
    for other in others:
        seen = other[(0,) * other.ndim]
        zero = zero + jnp.where(seen == seen, 0, 1)
    return zero


def on_device(
    pooled,
    cross_down,
    cross_up,
    cross_bias,
    comp_weight,
    comp_bias,
    over_weight,
    over_bias,
    table_tower,
    table_owner,
):
    tower_id, shard = lax.axis_index("tower"), lax.axis_index("shard")
    shards, towers = 16, 16
    _, batch, slot_most, emb = pooled.shape
    layers, rank, step = cross_up.shape[1:]
    features = step * shards
    width = comp_weight.shape[2]
    samples = batch // shards
    outputs = over_weight.shape[1] * shards

    anywhere = pl.BlockSpec(memory_space=pl.ANY)

    def whole(*shape):
        return pl.BlockSpec(shape, lambda i, *_: (0,) * len(shape))

    parts = (
        cross_down[0].reshape(layers * step, rank),
        cross_up[0].reshape(layers * rank, step),
        comp_weight[0],
    )
    packed_rows = sum(part.size for part in parts) // step
    packed = pl.pallas_call(
        pack_kernel,
        grid=(1,),
        in_specs=[anywhere] * len(parts),
        out_specs=whole(packed_rows, step),
        scratch_shapes=[pltpu.SemaphoreType.DMA((len(parts) + 1,))],
        out_shape=jax.ShapeDtypeStruct((packed_rows, step), BF16),
        compiler_params=pltpu.CompilerParams(vmem_limit_bytes=58 * 2**20),
    )(*parts)
    weights = lax.all_gather(packed, "shard", axis=0)

    over_rows = lax.all_gather(over_weight.T, "shard", axis=0, tiled=True)
    by_slot = pooled[0].transpose(1, 0, 2).reshape(slot_most, shards, samples, emb)

    def piece_for(to):
        return lax.dynamic_index_in_dim(by_slot, to % 16, 1, keepdims=False)

    pieces, zero, over_x, over_all = {0: piece_for(shard)}, once(over_rows), [over_rows], []
    for n in range(5):
        sent = []
        if n == 0:
            for d in range(1, 4):
                moves = [(i, (i + 4 * d) % 16) for i in range(16)]
                over_x.append(lax.ppermute(over_rows, "tower", moves))
            sent = over_x[1:]
        else:
            if n == 1:
                over_x = jnp.stack(over_x)
            part = lax.dynamic_index_in_dim(over_x, n - 1 + zero, 0, keepdims=False)
            over_all.append(part)
            for e in range(1, 4):
                moves = [(i, i // 4 * 4 + (i + e) % 4) for i in range(16)]
                sent.append(lax.ppermute(part, "tower", moves))
            over_all += sent
        for k in BACK[1 + 3 * n : 4 + 3 * n]:
            moves = [(i, (i + k) % 16) for i in range(16)]
            pieces[k] = lax.ppermute(piece_for(shard + k + zero), "shard", moves)
        zero = once(*sent, *[pieces[k] for k in BACK[1 + 3 * n : 4 + 3 * n]])
    pieces = [pieces[k] for k in BACK]

    slots = slot_order(table_tower, table_owner, tower_id, features // emb, slot_most)
    index = jnp.arange(shards * slot_most, dtype=jnp.int32)[:, None]
    turn = jnp.arange(1, slots.shape[0] + 1, dtype=jnp.int32)[None, :]
    places = jnp.sum(jnp.where(slots[None, :] == index, turn, 0), axis=1) - 1
    places = jnp.concatenate([places, (shard + zero)[None]]).astype(jnp.int32)

    tables = pl.pallas_call(
        table_kernel,
        grid_spec=pltpu.PrefetchScalarGridSpec(
            num_scalar_prefetch=1,
            grid=(1,),
            in_specs=[anywhere] * shards,
            out_specs=whole(samples, features),
            scratch_shapes=[pltpu.SemaphoreType.DMA],
        ),
        out_shape=jax.ShapeDtypeStruct((samples, features), BF16),
        compiler_params=pltpu.CompilerParams(vmem_limit_bytes=40 * 2**20),
        cost_estimate=pl.CostEstimate(flops=0, bytes_accessed=10 * 10**6, transcendentals=0),
    )(places, *pieces)

    squeezed = pl.pallas_call(
        tower_kernel,
        grid_spec=pl.GridSpec(
            grid=(1,),
            in_specs=[anywhere, anywhere, whole(layers, features), whole(1, width)],
            out_specs=whole(samples, width),
            scratch_shapes=[
                pltpu.VMEM((samples, features), BF16),
                pltpu.VMEM((samples, features), BF16),
                pltpu.VMEM((shards, step, rank), BF16),
                pltpu.VMEM((shards, step, rank), BF16),
                pltpu.VMEM((shards, rank, step), BF16),
                pltpu.VMEM((shards, rank, step), BF16),
                pltpu.VMEM((shards, step, width), BF16),
                pltpu.SemaphoreType.DMA((5 + 3 * QUARTERS,)),
            ],
        ),
        out_shape=jax.ShapeDtypeStruct((samples, width), BF16),
        compiler_params=pltpu.CompilerParams(vmem_limit_bytes=36 * 2**20),
        cost_estimate=pl.CostEstimate(flops=8 * 10**9, bytes_accessed=24 * 10**6, transcendentals=0),
    )(tables, weights, cross_bias[0].astype(F32), comp_bias.astype(F32))

    small = samples // towers
    joined = lax.all_to_all(squeezed.reshape(towers, small, width), "tower", 0, 0, tiled=True)
    place = jnp.stack([tower_id // 4, tower_id % 4]).astype(jnp.int32)
    scores = pl.pallas_call(
        over_kernel,
        grid_spec=pltpu.PrefetchScalarGridSpec(
            num_scalar_prefetch=1,
            grid=(1,),
            in_specs=[whole(towers, small, width)]
            + [anywhere] * towers
            + [whole(1, outputs)],
            out_specs=whole(small, outputs),
            scratch_shapes=[
                pltpu.VMEM((towers, outputs, width), BF16),
                pltpu.SemaphoreType.DMA((towers,)),
            ],
        ),
        out_shape=jax.ShapeDtypeStruct((small, outputs), BF16),
        compiler_params=pltpu.CompilerParams(vmem_limit_bytes=58 * 2**20),
        cost_estimate=pl.CostEstimate(flops=2 * 10**8, bytes_accessed=9 * 10**6, transcendentals=0),
    )(place, joined, *over_all, over_bias.astype(F32)[None])
    return scores[None]


def solution(mesh):
    placed = (
        P("tower", None, "shard", None),
        P("tower", None, "shard", None),
        P("tower", None, None, "shard"),
        P("tower", None, None),
        P("tower", "shard", None),
        P("tower", None),
        P("tower", "shard"),
        P(),
        P(),
        P(),
    )
    return jax.shard_map(
        on_device, mesh=mesh, in_specs=placed, out_specs=P("shard", "tower", None), check_vma=False
    )
```

```python
import jax
import jax.numpy as jnp
from jax import lax
from jax.experimental import pallas as pl
from jax.experimental.pallas import tpu as pltpu
from jax.sharding import PartitionSpec as P

F32 = jnp.float32
BF16 = jnp.bfloat16


def slot_order(table_tower, table_owner, tower_id, per_tower, slot_most):
    table_count = table_tower.shape[0]
    index = jnp.arange(table_count, dtype=jnp.int32)
    inside = table_tower == tower_id
    earlier = index[None, :] < index[:, None]
    before = inside[None, :] & earlier
    position_in = jnp.sum(before.astype(jnp.int32), axis=1)
    same_owner = table_owner[None, :] == table_owner[:, None]
    own_slot = jnp.sum((before & same_owner).astype(jnp.int32), axis=1)
    wanted = table_owner * slot_most + own_slot
    picked = inside[None, :] & (
        position_in[None, :] == jnp.arange(per_tower, dtype=jnp.int32)[:, None]
    )
    return jnp.sum(jnp.where(picked, wanted[None, :], 0), axis=1)


QUARTERS = 4
BACK = (0, 1, 7, 2, 6, 3, 5, 4)


def pack_kernel(down, up, comp, over, out, sems):
    half = out.shape[1]
    sources = [down.at[:, pl.ds(0, half)], down.at[:, pl.ds(half, half)], up, comp, over]
    copies, first = [], 0
    for n, source in enumerate(sources):
        count = source.shape[0]
        copies.append(pltpu.make_async_copy(source, out.at[pl.ds(first, count), :], sems.at[n]))
        first += count
    for copy in copies:
        copy.start()
    for copy in copies:
        copy.wait()


def table_kernel(places, *refs):
    pieces, (base, sem) = refs[:-2], refs[-2:]
    shards, slot_most = len(pieces), pieces[0].shape[0]
    me = places[shards * slot_most]
    z, core = me // 2, lax.rem(me, 2)
    for k in range(shards):
        plane = lax.rem(z + 8 - BACK[k // 2], 8)
        owner = 2 * plane + (core if k % 2 == 0 else 1 - core)
        for slot in range(slot_most):
            place = places[owner * slot_most + slot]

            @pl.when(place >= 0)
            def _(k=k, slot=slot, place=place):
                pltpu.make_async_copy(
                    pieces[k].at[slot],
                    base.at[:, pl.ds(pl.multiple_of(place * 128, 128), 128)],
                    sem,
                ).start()

    pltpu.make_async_copy(base, base, sem).wait()


def tower_kernel(
    tables, weights, bias, comp_bias, out, base, state, down0, down1, up0, up1, comp, over, sems
):
    features = base.shape[1]
    shards, step, rank = down0.shape
    width = comp.shape[2]
    block, half = shards // QUARTERS, rank // 2

    def bring(first, count, target, n):
        return pltpu.make_async_copy(weights.at[:, pl.ds(first, count), :], target, sems.at[n])

    early = []
    for q in range(QUARTERS):
        there, columns = pl.ds(q * block, block), pl.ds(q * block * step, block * step)
        early.append(
            pltpu.make_async_copy(tables.at[:, columns], base.at[:, columns], sems.at[3 * q])
        )
        for h in range(2):
            early.append(
                pltpu.make_async_copy(
                    weights.at[there, pl.ds(2 * step * h, step), :],
                    down0.at[there, :, pl.ds(h * half, half)],
                    sems.at[3 * q + 1 + h],
                )
            )
    n, at_up = 3 * QUARTERS, 4 * step
    bring_up0 = bring(at_up, rank, up0, n)
    bring_down1 = [
        bring(2 * step * h + step, step, down1.at[:, :, pl.ds(h * half, half)], n + 1 + h)
        for h in range(2)
    ]
    bring_up1 = bring(at_up + rank, rank, up1, n + 3)
    bring_comp = bring(at_up + 2 * rank, step, comp, n + 4)
    bring_over = bring(at_up + 2 * rank + step, over.shape[1], over, n + 5)
    for copy in (*early, bring_up0, *bring_down1, bring_up1, bring_comp, bring_over):
        copy.start()

    total = None
    for q in range(QUARTERS):
        for copy in early[3 * q : 3 * q + 3]:
            copy.wait()
        deep = block * step
        part = jnp.dot(
            base[:, pl.ds(q * deep, deep)],
            down0.reshape(features, rank)[pl.ds(q * deep, deep), :],
            preferred_element_type=F32,
        )
        total = part if total is None else total + part
    lowered = total.astype(BF16)
    bring_up0.wait()
    for s in range(shards):
        here = pl.ds(s * step, step)
        raised = jnp.dot(lowered, up0[s], preferred_element_type=F32)
        part = base[:, here].astype(F32)
        state[:, here] = (part * (raised + bias[0:1, here]) + part).astype(BF16)
    bring_down1[0].wait()
    bring_down1[1].wait()
    lowered = jnp.dot(
        state[...], down1.reshape(features, rank)[...], preferred_element_type=F32
    ).astype(BF16)
    bring_up1.wait()
    for s in range(shards):
        here = pl.ds(s * step, step)
        raised = jnp.dot(lowered, up1[s], preferred_element_type=F32)
        part, held = base[:, here].astype(F32), state[:, here].astype(F32)
        state[:, here] = (part * (raised + bias[1:2, here]) + held).astype(BF16)
    bring_comp.wait()
    squeezed = jnp.dot(state[...], comp.reshape(features, width)[...], preferred_element_type=F32)
    squeezed = (squeezed + comp_bias[...]).astype(BF16)
    bring_over.wait()
    over_t = over.reshape(over.shape[0] * over.shape[1], width)[...]
    out[...] = lax.dot_general(
        squeezed, over_t, (((1,), (1,)), ((), ())), preferred_element_type=F32
    ).astype(BF16)


def on_device(
    pooled,
    cross_down,
    cross_up,
    cross_bias,
    comp_weight,
    comp_bias,
    over_weight,
    over_bias,
    table_tower,
    table_owner,
):
    tower_id, shard = lax.axis_index("tower"), lax.axis_index("shard")
    shards, towers = 16, 16
    _, batch, slot_most, emb = pooled.shape
    layers, rank, step = cross_up.shape[1:]
    features = step * shards
    width = comp_weight.shape[2]
    samples = batch // shards
    columns = over_weight.shape[1]
    outputs = columns * shards

    anywhere = pl.BlockSpec(memory_space=pl.ANY)

    def whole(*shape):
        return pl.BlockSpec(shape, lambda i, *_: (0,) * len(shape))

    parts = (
        cross_down[0].reshape(layers * step, rank),
        cross_up[0].reshape(layers * rank, step),
        comp_weight[0],
        over_weight.T,
    )
    packed_rows = sum(part.size for part in parts) // step
    packed = pl.pallas_call(
        pack_kernel,
        grid=(1,),
        in_specs=[anywhere] * len(parts),
        out_specs=whole(packed_rows, step),
        scratch_shapes=[pltpu.SemaphoreType.DMA((len(parts) + 1,))],
        out_shape=jax.ShapeDtypeStruct((packed_rows, step), BF16),
        compiler_params=pltpu.CompilerParams(vmem_limit_bytes=58 * 2**20),
    )(*parts)
    weights = lax.all_gather(packed, "shard", axis=0)

    z, core = shard // 2, shard % 2
    by_slot = pooled[0].transpose(1, 0, 2).reshape(slot_most, 8, 2, samples, emb)
    swap = [(i, i ^ 1) for i in range(16)]
    pieces = []
    for k in BACK:
        both = lax.dynamic_index_in_dim(by_slot, (z + k) % 8, 1, keepdims=False)
        if k:
            moves = [(i, (i + 2 * k) % 16) for i in range(16)]
            both = lax.ppermute(both, "shard", moves)
        pieces.append(lax.dynamic_index_in_dim(both, core, 1, keepdims=False))
        theirs = lax.dynamic_index_in_dim(both, 1 - core, 1, keepdims=False)
        pieces.append(lax.ppermute(theirs, "shard", swap))

    slots = slot_order(table_tower, table_owner, tower_id, features // emb, slot_most)
    index = jnp.arange(shards * slot_most, dtype=jnp.int32)[:, None]
    turn = jnp.arange(1, slots.shape[0] + 1, dtype=jnp.int32)[None, :]
    places = jnp.sum(jnp.where(slots[None, :] == index, turn, 0), axis=1) - 1
    places = jnp.concatenate([places, shard[None]]).astype(jnp.int32)

    tables = pl.pallas_call(
        table_kernel,
        grid_spec=pltpu.PrefetchScalarGridSpec(
            num_scalar_prefetch=1,
            grid=(1,),
            in_specs=[anywhere] * shards,
            out_specs=whole(samples, features),
            scratch_shapes=[pltpu.SemaphoreType.DMA],
        ),
        out_shape=jax.ShapeDtypeStruct((samples, features), BF16),
        compiler_params=pltpu.CompilerParams(vmem_limit_bytes=12 * 2**20),
        cost_estimate=pl.CostEstimate(flops=0, bytes_accessed=10 * 10**6, transcendentals=0),
    )(places, *pieces)

    partial = pl.pallas_call(
        tower_kernel,
        grid_spec=pl.GridSpec(
            grid=(1,),
            in_specs=[anywhere, anywhere, whole(layers, features), whole(1, width)],
            out_specs=whole(samples, outputs),
            scratch_shapes=[
                pltpu.VMEM((samples, features), BF16),
                pltpu.VMEM((samples, features), BF16),
                pltpu.VMEM((shards, step, rank), BF16),
                pltpu.VMEM((shards, step, rank), BF16),
                pltpu.VMEM((shards, rank, step), BF16),
                pltpu.VMEM((shards, rank, step), BF16),
                pltpu.VMEM((shards, step, width), BF16),
                pltpu.VMEM((shards, columns, width), BF16),
                pltpu.SemaphoreType.DMA((6 + 3 * QUARTERS,)),
            ],
        ),
        out_shape=jax.ShapeDtypeStruct((samples, outputs), BF16),
        compiler_params=pltpu.CompilerParams(vmem_limit_bytes=36 * 2**20),
        cost_estimate=pl.CostEstimate(flops=8 * 10**9, bytes_accessed=24 * 10**6, transcendentals=0),
    )(tables, weights, cross_bias[0].astype(F32), comp_bias.astype(F32))

    summed = lax.all_to_all(
        partial.reshape(towers, samples // towers, outputs), "tower", 0, 0, tiled=True
    )
    total = jnp.sum(summed.astype(F32), axis=0) + over_bias.astype(F32)
    return jax.nn.relu(total).astype(BF16)[None]


def solution(mesh):
    placed = (
        P("tower", None, "shard", None),
        P("tower", None, "shard", None),
        P("tower", None, None, "shard"),
        P("tower", None, None),
        P("tower", "shard", None),
        P("tower", None),
        P("tower", "shard"),
        P(),
        P(),
        P(),
    )
    return jax.shard_map(
        on_device, mesh=mesh, in_specs=placed, out_specs=P("shard", "tower", None), check_vma=False
    )
```

```python
import jax
import jax.numpy as jnp
from jax import lax
from jax.experimental import pallas as pl
from jax.experimental.pallas import tpu as pltpu
from jax.sharding import PartitionSpec as P

F32 = jnp.float32
BF16 = jnp.bfloat16


def slot_order(table_tower, table_owner, tower_id, per_tower, slot_most):
    table_count = table_tower.shape[0]
    index = jnp.arange(table_count, dtype=jnp.int32)
    inside = table_tower == tower_id
    earlier = index[None, :] < index[:, None]
    before = inside[None, :] & earlier
    position_in = jnp.sum(before.astype(jnp.int32), axis=1)
    same_owner = table_owner[None, :] == table_owner[:, None]
    own_slot = jnp.sum((before & same_owner).astype(jnp.int32), axis=1)
    wanted = table_owner * slot_most + own_slot
    picked = inside[None, :] & (
        position_in[None, :] == jnp.arange(per_tower, dtype=jnp.int32)[:, None]
    )
    return jnp.sum(jnp.where(picked, wanted[None, :], 0), axis=1)


PARTS = 8
BACK = (0, 1, 7, 2, 6, 3, 5, 4)


def pack_kernel(down, up, comp, over, out, sems):
    half = out.shape[1]
    sources = [down.at[:, pl.ds(0, half)], down.at[:, pl.ds(half, half)], up, comp, over]
    copies, first = [], 0
    for n, source in enumerate(sources):
        count = source.shape[0]
        copies.append(pltpu.make_async_copy(source, out.at[pl.ds(first, count), :], sems.at[n]))
        first += count
    for copy in copies:
        copy.start()
    for copy in copies:
        copy.wait()


def table_kernel(places, *refs):
    pieces, (base, sem) = refs[:-2], refs[-2:]
    shards, slot_most = len(pieces), pieces[0].shape[0]
    me = places[shards * slot_most]
    z, core = me // 2, lax.rem(me, 2)
    for k in range(shards):
        plane = lax.rem(z + 8 - BACK[k // 2], 8)
        owner = 2 * plane + (core if k % 2 == 0 else 1 - core)
        for slot in range(slot_most):
            place = places[owner * slot_most + slot]

            @pl.when(place >= 0)
            def _(k=k, slot=slot, place=place):
                pltpu.make_async_copy(
                    pieces[k].at[slot],
                    base.at[:, pl.ds(pl.multiple_of(place * 128, 128), 128)],
                    sem,
                ).start()

    pltpu.make_async_copy(base, base, sem).wait()


def tower_kernel(
    tables, weights, bias, comp_bias, out, base, state, down0, down1, up0, up1, comp, over, sems
):
    features = base.shape[1]
    shards, step, rank = down0.shape
    width = comp.shape[2]
    block, half = shards // PARTS, rank // 2

    def bring(first, count, target, n):
        return pltpu.make_async_copy(weights.at[:, pl.ds(first, count), :], target, sems.at[n])

    early = []
    for q in range(PARTS):
        there, columns = pl.ds(q * block, block), pl.ds(q * block * step, block * step)
        early.append(
            pltpu.make_async_copy(tables.at[:, columns], base.at[:, columns], sems.at[3 * q])
        )
        for h in range(2):
            early.append(
                pltpu.make_async_copy(
                    weights.at[there, pl.ds(2 * step * h, step), :],
                    down0.at[there, :, pl.ds(h * half, half)],
                    sems.at[3 * q + 1 + h],
                )
            )
    n, at_up = 3 * PARTS, 4 * step
    bring_up0 = []
    for q in range(4):
        there = pl.ds(q * shards // 4, shards // 4)
        bring_up0.append(
            pltpu.make_async_copy(
                weights.at[there, pl.ds(at_up, rank), :], up0.at[there], sems.at[n + 5 + q]
            )
        )
    bring_down1 = [
        bring(2 * step * h + step, step, down1.at[:, :, pl.ds(h * half, half)], n + 1 + h)
        for h in range(2)
    ]
    bring_up1 = bring(at_up + rank, rank, up1, n + 3)
    bring_comp = bring(at_up + 2 * rank, step, comp, n + 4)
    bring_over = bring(at_up + 2 * rank + step, over.shape[1], over, n)
    for copy in (*early, *bring_up0, *bring_down1, bring_up1, bring_comp, bring_over):
        copy.start()

    total = None
    for q in range(PARTS):
        for copy in early[3 * q : 3 * q + 3]:
            copy.wait()
        deep = block * step
        part = jnp.dot(
            base[:, pl.ds(q * deep, deep)],
            down0.reshape(features, rank)[pl.ds(q * deep, deep), :],
            preferred_element_type=F32,
        )
        total = part if total is None else total + part
    lowered = total.astype(BF16)
    for s in range(shards):
        if s % (shards // 4) == 0:
            bring_up0[s // (shards // 4)].wait()
        here = pl.ds(s * step, step)
        raised = jnp.dot(lowered, up0[s], preferred_element_type=F32)
        part = base[:, here].astype(F32)
        state[:, here] = (part * (raised + bias[0:1, here]) + part).astype(BF16)
    bring_down1[0].wait()
    bring_down1[1].wait()
    lowered = jnp.dot(
        state[...], down1.reshape(features, rank)[...], preferred_element_type=F32
    ).astype(BF16)
    bring_up1.wait()
    for s in range(shards):
        here = pl.ds(s * step, step)
        raised = jnp.dot(lowered, up1[s], preferred_element_type=F32)
        part, held = base[:, here].astype(F32), state[:, here].astype(F32)
        state[:, here] = (part * (raised + bias[1:2, here]) + held).astype(BF16)
    bring_comp.wait()
    squeezed = jnp.dot(state[...], comp.reshape(features, width)[...], preferred_element_type=F32)
    squeezed = (squeezed + comp_bias[...]).astype(BF16)
    bring_over.wait()
    over_t = over.reshape(over.shape[0] * over.shape[1], width)[...]
    out[...] = lax.dot_general(
        squeezed, over_t, (((1,), (1,)), ((), ())), preferred_element_type=F32
    ).astype(BF16)


def on_device(
    pooled,
    cross_down,
    cross_up,
    cross_bias,
    comp_weight,
    comp_bias,
    over_weight,
    over_bias,
    table_tower,
    table_owner,
):
    tower_id, shard = lax.axis_index("tower"), lax.axis_index("shard")
    shards, towers = 16, 16
    _, batch, slot_most, emb = pooled.shape
    layers, rank, step = cross_up.shape[1:]
    features = step * shards
    width = comp_weight.shape[2]
    samples = batch // shards
    columns = over_weight.shape[1]
    outputs = columns * shards

    anywhere = pl.BlockSpec(memory_space=pl.ANY)

    def whole(*shape):
        return pl.BlockSpec(shape, lambda i, *_: (0,) * len(shape))

    parts = (
        cross_down[0].reshape(layers * step, rank),
        cross_up[0].reshape(layers * rank, step),
        comp_weight[0],
        over_weight.T,
    )
    packed_rows = sum(part.size for part in parts) // step
    packed = pl.pallas_call(
        pack_kernel,
        grid=(1,),
        in_specs=[anywhere] * len(parts),
        out_specs=whole(packed_rows, step),
        scratch_shapes=[pltpu.SemaphoreType.DMA((len(parts) + 1,))],
        out_shape=jax.ShapeDtypeStruct((packed_rows, step), BF16),
        compiler_params=pltpu.CompilerParams(vmem_limit_bytes=58 * 2**20),
    )(*parts)
    weights = lax.all_gather(packed, "shard", axis=0)

    z, core = shard // 2, shard % 2
    by_slot = pooled[0].transpose(1, 0, 2).reshape(slot_most, 8, 2, samples, emb)
    swap = [(i, i ^ 1) for i in range(16)]
    pieces = []
    for k in BACK:
        both = lax.dynamic_index_in_dim(by_slot, (z + k) % 8, 1, keepdims=False)
        if k:
            moves = [(i, (i + 2 * k) % 16) for i in range(16)]
            both = lax.ppermute(both, "shard", moves)
        pieces.append(lax.dynamic_index_in_dim(both, core, 1, keepdims=False))
        theirs = lax.dynamic_index_in_dim(both, 1 - core, 1, keepdims=False)
        pieces.append(lax.ppermute(theirs, "shard", swap))

    slots = slot_order(table_tower, table_owner, tower_id, features // emb, slot_most)
    index = jnp.arange(shards * slot_most, dtype=jnp.int32)[:, None]
    turn = jnp.arange(1, slots.shape[0] + 1, dtype=jnp.int32)[None, :]
    places = jnp.sum(jnp.where(slots[None, :] == index, turn, 0), axis=1) - 1
    places = jnp.concatenate([places, shard[None]]).astype(jnp.int32)

    tables = pl.pallas_call(
        table_kernel,
        grid_spec=pltpu.PrefetchScalarGridSpec(
            num_scalar_prefetch=1,
            grid=(1,),
            in_specs=[anywhere] * shards,
            out_specs=whole(samples, features),
            scratch_shapes=[pltpu.SemaphoreType.DMA],
        ),
        out_shape=jax.ShapeDtypeStruct((samples, features), BF16),
        compiler_params=pltpu.CompilerParams(vmem_limit_bytes=12 * 2**20),
        cost_estimate=pl.CostEstimate(flops=0, bytes_accessed=10 * 10**6, transcendentals=0),
    )(places, *pieces)

    partial = pl.pallas_call(
        tower_kernel,
        grid_spec=pl.GridSpec(
            grid=(1,),
            in_specs=[anywhere, anywhere, whole(layers, features), whole(1, width)],
            out_specs=whole(samples, outputs),
            scratch_shapes=[
                pltpu.VMEM((samples, features), BF16),
                pltpu.VMEM((samples, features), BF16),
                pltpu.VMEM((shards, step, rank), BF16),
                pltpu.VMEM((shards, step, rank), BF16),
                pltpu.VMEM((shards, rank, step), BF16),
                pltpu.VMEM((shards, rank, step), BF16),
                pltpu.VMEM((shards, step, width), BF16),
                pltpu.VMEM((shards, columns, width), BF16),
                pltpu.SemaphoreType.DMA((9 + 3 * PARTS,)),
            ],
        ),
        out_shape=jax.ShapeDtypeStruct((samples, outputs), BF16),
        compiler_params=pltpu.CompilerParams(vmem_limit_bytes=36 * 2**20),
        cost_estimate=pl.CostEstimate(flops=8 * 10**9, bytes_accessed=24 * 10**6, transcendentals=0),
    )(tables, weights, cross_bias[0].astype(F32), comp_bias.astype(F32))

    summed = lax.all_to_all(
        partial.reshape(towers, samples // towers, outputs), "tower", 0, 0, tiled=True
    )
    total = jnp.sum(summed.astype(F32), axis=0) + over_bias.astype(F32)
    return jax.nn.relu(total).astype(BF16)[None]


def solution(mesh):
    placed = (
        P("tower", None, "shard", None),
        P("tower", None, "shard", None),
        P("tower", None, None, "shard"),
        P("tower", None, None),
        P("tower", "shard", None),
        P("tower", None),
        P("tower", "shard"),
        P(),
        P(),
        P(),
    )
    return jax.shard_map(
        on_device, mesh=mesh, in_specs=placed, out_specs=P("shard", "tower", None), check_vma=False
    )
```

```python
import jax
import jax.numpy as jnp
from jax import lax
from jax.experimental import pallas as pl
from jax.experimental.pallas import tpu as pltpu
from jax.sharding import PartitionSpec as P

F32 = jnp.float32
BF16 = jnp.bfloat16


def slot_order(table_tower, table_owner, tower_id, per_tower, slot_most):
    table_count = table_tower.shape[0]
    index = jnp.arange(table_count, dtype=jnp.int32)
    inside = table_tower == tower_id
    earlier = index[None, :] < index[:, None]
    before = inside[None, :] & earlier
    position_in = jnp.sum(before.astype(jnp.int32), axis=1)
    same_owner = table_owner[None, :] == table_owner[:, None]
    own_slot = jnp.sum((before & same_owner).astype(jnp.int32), axis=1)
    wanted = table_owner * slot_most + own_slot
    picked = inside[None, :] & (
        position_in[None, :] == jnp.arange(per_tower, dtype=jnp.int32)[:, None]
    )
    return jnp.sum(jnp.where(picked, wanted[None, :], 0), axis=1)


PARTS = 2
BACK = (0, 1, 7, 2, 6, 3, 5, 4)


def pack_kernel(down, up, comp, over, out, sems):
    half = out.shape[1]
    sources = [down.at[:, pl.ds(0, half)], down.at[:, pl.ds(half, half)], up, comp, over]
    copies, first = [], 0
    for n, source in enumerate(sources):
        count = source.shape[0]
        copies.append(pltpu.make_async_copy(source, out.at[pl.ds(first, count), :], sems.at[n]))
        first += count
    for copy in copies:
        copy.start()
    for copy in copies:
        copy.wait()


def table_kernel(places, *refs):
    pieces, (base, sem) = refs[:-2], refs[-2:]
    shards, slot_most = len(pieces), pieces[0].shape[0]
    me = places[shards * slot_most]
    z, core = me // 2, lax.rem(me, 2)
    for k in range(shards):
        plane = lax.rem(z + 8 - BACK[k // 2], 8)
        owner = 2 * plane + (core if k % 2 == 0 else 1 - core)
        for slot in range(slot_most):
            place = places[owner * slot_most + slot]

            @pl.when(place >= 0)
            def _(k=k, slot=slot, place=place):
                pltpu.make_async_copy(
                    pieces[k].at[slot],
                    base.at[:, pl.ds(pl.multiple_of(place * 128, 128), 128)],
                    sem,
                ).start()

    pltpu.make_async_copy(base, base, sem).wait()


def tower_kernel(
    tables, weights, bias, comp_bias, out, base, state, down0, down1, up0, up1, comp, over, sems
):
    features = base.shape[1]
    shards, step, rank = down0.shape
    width = comp.shape[2]
    block, half = shards // PARTS, rank // 2

    def bring(first, count, target, n):
        return pltpu.make_async_copy(weights.at[:, pl.ds(first, count), :], target, sems.at[n])

    early = []
    for q in range(PARTS):
        there, columns = pl.ds(q * block, block), pl.ds(q * block * step, block * step)
        early.append(
            pltpu.make_async_copy(tables.at[:, columns], base.at[:, columns], sems.at[3 * q])
        )
        for h in range(2):
            early.append(
                pltpu.make_async_copy(
                    weights.at[there, pl.ds(2 * step * h, step), :],
                    down0.at[there, :, pl.ds(h * half, half)],
                    sems.at[3 * q + 1 + h],
                )
            )
    n, at_up = 3 * PARTS, 4 * step
    bring_up0 = bring(at_up, rank, up0, n)
    bring_down1 = [
        bring(2 * step * h + step, step, down1.at[:, :, pl.ds(h * half, half)], n + 1 + h)
        for h in range(2)
    ]
    bring_up1 = bring(at_up + rank, rank, up1, n + 3)
    bring_comp = bring(at_up + 2 * rank, step, comp, n + 4)
    bring_over = bring(at_up + 2 * rank + step, over.shape[1], over, n + 5)
    for copy in (*early, bring_up0, *bring_down1, bring_up1, bring_comp, bring_over):
        copy.start()

    total = None
    for q in range(PARTS):
        for copy in early[3 * q : 3 * q + 3]:
            copy.wait()
        deep = block * step
        part = jnp.dot(
            base[:, pl.ds(q * deep, deep)],
            down0.reshape(features, rank)[pl.ds(q * deep, deep), :],
            preferred_element_type=F32,
        )
        total = part if total is None else total + part
    lowered = total.astype(BF16)
    bring_up0.wait()
    for s in range(shards):
        here = pl.ds(s * step, step)
        raised = jnp.dot(lowered, up0[s], preferred_element_type=F32)
        part = base[:, here].astype(F32)
        state[:, here] = (part * (raised + bias[0:1, here]) + part).astype(BF16)
    bring_down1[0].wait()
    bring_down1[1].wait()
    lowered = jnp.dot(
        state[...], down1.reshape(features, rank)[...], preferred_element_type=F32
    ).astype(BF16)
    bring_up1.wait()
    for s in range(shards):
        here = pl.ds(s * step, step)
        raised = jnp.dot(lowered, up1[s], preferred_element_type=F32)
        part, held = base[:, here].astype(F32), state[:, here].astype(F32)
        state[:, here] = (part * (raised + bias[1:2, here]) + held).astype(BF16)
    bring_comp.wait()
    squeezed = jnp.dot(state[...], comp.reshape(features, width)[...], preferred_element_type=F32)
    squeezed = (squeezed + comp_bias[...]).astype(BF16)
    bring_over.wait()
    over_t = over.reshape(over.shape[0] * over.shape[1], width)[...]
    out[...] = lax.dot_general(
        squeezed, over_t, (((1,), (1,)), ((), ())), preferred_element_type=F32
    ).astype(BF16)


def on_device(
    pooled,
    cross_down,
    cross_up,
    cross_bias,
    comp_weight,
    comp_bias,
    over_weight,
    over_bias,
    table_tower,
    table_owner,
):
    tower_id, shard = lax.axis_index("tower"), lax.axis_index("shard")
    shards, towers = 16, 16
    _, batch, slot_most, emb = pooled.shape
    layers, rank, step = cross_up.shape[1:]
    features = step * shards
    width = comp_weight.shape[2]
    samples = batch // shards
    columns = over_weight.shape[1]
    outputs = columns * shards

    anywhere = pl.BlockSpec(memory_space=pl.ANY)

    def whole(*shape):
        return pl.BlockSpec(shape, lambda i, *_: (0,) * len(shape))

    parts = (
        cross_down[0].reshape(layers * step, rank),
        cross_up[0].reshape(layers * rank, step),
        comp_weight[0],
        over_weight.T,
    )
    packed_rows = sum(part.size for part in parts) // step
    packed = pl.pallas_call(
        pack_kernel,
        grid=(1,),
        in_specs=[anywhere] * len(parts),
        out_specs=whole(packed_rows, step),
        scratch_shapes=[pltpu.SemaphoreType.DMA((len(parts) + 1,))],
        out_shape=jax.ShapeDtypeStruct((packed_rows, step), BF16),
        compiler_params=pltpu.CompilerParams(vmem_limit_bytes=58 * 2**20),
    )(*parts)
    weights = lax.all_gather(packed, "shard", axis=0)

    z, core = shard // 2, shard % 2
    by_slot = pooled[0].transpose(1, 0, 2).reshape(slot_most, 8, 2, samples, emb)
    swap = [(i, i ^ 1) for i in range(16)]
    pieces = []
    for k in BACK:
        both = lax.dynamic_index_in_dim(by_slot, (z + k) % 8, 1, keepdims=False)
        if k:
            moves = [(i, (i + 2 * k) % 16) for i in range(16)]
            both = lax.ppermute(both, "shard", moves)
        pieces.append(lax.dynamic_index_in_dim(both, core, 1, keepdims=False))
        theirs = lax.dynamic_index_in_dim(both, 1 - core, 1, keepdims=False)
        pieces.append(lax.ppermute(theirs, "shard", swap))

    slots = slot_order(table_tower, table_owner, tower_id, features // emb, slot_most)
    index = jnp.arange(shards * slot_most, dtype=jnp.int32)[:, None]
    turn = jnp.arange(1, slots.shape[0] + 1, dtype=jnp.int32)[None, :]
    places = jnp.sum(jnp.where(slots[None, :] == index, turn, 0), axis=1) - 1
    places = jnp.concatenate([places, shard[None]]).astype(jnp.int32)

    tables = pl.pallas_call(
        table_kernel,
        grid_spec=pltpu.PrefetchScalarGridSpec(
            num_scalar_prefetch=1,
            grid=(1,),
            in_specs=[anywhere] * shards,
            out_specs=whole(samples, features),
            scratch_shapes=[pltpu.SemaphoreType.DMA],
        ),
        out_shape=jax.ShapeDtypeStruct((samples, features), BF16),
        compiler_params=pltpu.CompilerParams(vmem_limit_bytes=12 * 2**20),
        cost_estimate=pl.CostEstimate(flops=0, bytes_accessed=10 * 10**6, transcendentals=0),
    )(places, *pieces)

    partial = pl.pallas_call(
        tower_kernel,
        grid_spec=pl.GridSpec(
            grid=(1,),
            in_specs=[anywhere, anywhere, whole(layers, features), whole(1, width)],
            out_specs=whole(samples, outputs),
            scratch_shapes=[
                pltpu.VMEM((samples, features), BF16),
                pltpu.VMEM((samples, features), BF16),
                pltpu.VMEM((shards, step, rank), BF16),
                pltpu.VMEM((shards, step, rank), BF16),
                pltpu.VMEM((shards, rank, step), BF16),
                pltpu.VMEM((shards, rank, step), BF16),
                pltpu.VMEM((shards, step, width), BF16),
                pltpu.VMEM((shards, columns, width), BF16),
                pltpu.SemaphoreType.DMA((6 + 3 * PARTS,)),
            ],
        ),
        out_shape=jax.ShapeDtypeStruct((samples, outputs), BF16),
        compiler_params=pltpu.CompilerParams(vmem_limit_bytes=36 * 2**20),
        cost_estimate=pl.CostEstimate(flops=8 * 10**9, bytes_accessed=24 * 10**6, transcendentals=0),
    )(tables, weights, cross_bias[0].astype(F32), comp_bias.astype(F32))

    summed = lax.all_to_all(
        partial.reshape(towers, samples // towers, outputs), "tower", 0, 0, tiled=True
    )
    total = jnp.sum(summed.astype(F32), axis=0) + over_bias.astype(F32)
    return jax.nn.relu(total).astype(BF16)[None]


def solution(mesh):
    placed = (
        P("tower", None, "shard", None),
        P("tower", None, "shard", None),
        P("tower", None, None, "shard"),
        P("tower", None, None),
        P("tower", "shard", None),
        P("tower", None),
        P("tower", "shard"),
        P(),
        P(),
        P(),
    )
    return jax.shard_map(
        on_device, mesh=mesh, in_specs=placed, out_specs=P("shard", "tower", None), check_vma=False
    )
```
